512 devices in a mesh: dp: 128 (over y_hi, z, x), tensor: 4 (over y_lo, core).
Axes of the slice: x: 4, y: 4 (y_hi: 2, y_lo: 2; y = y_hi * 2 + y_lo), z: 16, core: 2. Of those that a mesh axis runs over, the one named last changes fastest.
Arguments:
- rows_in: bfloat16 [32768, 1152], P('dp'), may hold values from -6 to 6
- patch_counts: int32 [128, 2], P('dp'), may hold values from 32 to 128, as said below
- row_slots: int32 [128, 256], P('dp'), may hold values from 0 to 255, each once within a row
- w_qkv: bfloat16 [1152, 3456], P(None, 'tensor'), may hold values from -0.1875 to 0.1875
- w_out: bfloat16 [1152, 1152], P('tensor'), may hold values from -0.1875 to 0.1875
- w_fc1: bfloat16 [1152, 4304], P(None, 'tensor'), may hold values from -0.1875 to 0.1875
- w_fc2: bfloat16 [4304, 1152], P('tensor'), may hold values from -0.09375 to 0.09375
- text_embeds: bfloat16 [256, 1152], P('dp'), may hold values from -6 to 6
- similarity_multiplier: float32 [1], replicated, may hold values from 2 to 8
- similarity_shift_term: float32 [1], replicated, may hold values from -6 to -2
Outputs:
- rows_out: bfloat16 [32768, 1152], P('dp')
- pooled_grad: float32 [256, 1152], P('dp')
The draws below stay inside these ranges and needn't reach their ends.
Inputs may be any that keep to these rules, and one draw needn't show every extreme that they name: `patch_counts`: each device's 2 images fill its first rows one after another; the remaining rows are padding. Both bounds are reached in every draw. Each device's row of row_slots is a permutation of 0 to 255.
All inputs are finite; a program needn't handle non-finite values.
Results may differ from the reference program's by a relative error of at most 0.015.
Values may be sent and summed in bfloat16 or wider, within the bound.
No kernel may reach another device: no remote copies, remote signals or barrier semaphores. Data moves between devices by JAX's collectives and lax.ppermute only.
A program may use at most 64 MiB of HBM per device.

```python
import math
from functools import partial
import jax
import jax.numpy as jnp
from jax import lax

D = 1152
FF = 4304
HEAD_DIM = 72
ROWS = 256
IMG_DEV = 2
SLOT = 2
IMAGES = 256
N_DP = 128
N_TENSOR = 4


def draw_patch_counts(key, part):
    key = jax.random.fold_in(key, 11)
    most_rows = ROWS // IMG_DEV
    fewest_rows = most_rows // 4
    counts = jax.random.randint(key, (N_DP, IMG_DEV), fewest_rows, most_rows + 1)
    counts = counts.at[0, 0].set(most_rows)
    counts = counts.at[N_DP - 1, IMG_DEV - 1].set(fewest_rows)
    return counts.astype(jnp.int32)


def level_of(key, dims, cuts, least, high):
    level = 1.0
    for position, shards_of in cuts:
        steps = jax.random.uniform(jax.random.fold_in(jax.random.fold_in(key, 6), position), (shards_of,), jnp.float32, least / len(cuts), high / len(cuts))
        level = level * jnp.repeat(jnp.exp(steps), dims[position] // shards_of).reshape((-1,) + (1,) * (len(dims) - 1 - position))
    return level


def gaussian(own_key, extent, deviation, reach, cuts=(), kind=jnp.bfloat16):
    array = deviation * jax.random.normal(own_key, extent, jnp.float32)
    if cuts:
        array = array * level_of(own_key, extent, cuts, -0.22, 0.18)
    return jnp.clip(array, -reach, reach).astype(kind)


def setup_inputs(seed: int = 0) -> dict:
    seeds = jax.random.split(jax.random.key(seed), 11)
    return {
        "rows_in": gaussian(seeds[0], (N_DP * ROWS, D), 1.0, 6.0, ((0, 128),)),
        "patch_counts": draw_patch_counts(jax.random.fold_in(seeds[10], 71), 0),
        "row_slots": jax.vmap(lambda own: jax.random.permutation(own, ROWS))(jax.random.split(seeds[2], N_DP)).reshape((N_DP, ROWS)).astype(jnp.int32),
        "w_qkv": gaussian(seeds[3], (D, 3 * D), D ** -0.5, 0.1875, ((1, 4),)),
        "w_out": gaussian(seeds[4], (D, D), D ** -0.5, 0.1875, ((0, 4),)),
        "w_fc1": gaussian(seeds[5], (D, FF), D ** -0.5, 0.1875, ((1, 4),)),
        "w_fc2": gaussian(seeds[6], (FF, D), FF ** -0.5, 0.09375, ((0, 4),)),
        "text_embeds": gaussian(seeds[7], (IMAGES, D), 1.0, 6.0, ((0, 128),)),
        "similarity_multiplier": jnp.clip(jnp.exp(jax.random.uniform(seeds[8], (1,), jnp.float32, math.log(2.0), math.log(8.0))), 2.0, 8.0),
        "similarity_shift_term": jnp.clip(jax.random.uniform(seeds[9], (1,), jnp.float32, -6.0, -2.0), -6.0, -2.0),
    }


def layer_norm(values):
    mean_val = lax.optimization_barrier(jnp.mean(values, axis=-1, keepdims=True))
    centred = values - mean_val
    var_val = lax.optimization_barrier(jnp.mean(centred * centred, axis=-1, keepdims=True))
    return centred * lax.rsqrt(var_val + 1e-06)

def one_device(pieces, w_qkv, w_out, w_fc1, w_fc2):
    rows_here, counts = pieces
    row_count = rows_here.shape[0]
    head_count = D // HEAD_DIM
    group_heads = head_count // N_TENSOR
    bounds = jnp.cumsum(counts).astype(jnp.int32)
    positions = jnp.arange(row_count, dtype=jnp.int32)
    segment = lax.optimization_barrier(jnp.sum((positions[:, None] >= bounds[None, :]).astype(jnp.int32), axis=1))
    normed = layer_norm(rows_here.astype(jnp.float32)).astype(jnp.bfloat16)
    projected = jnp.dot(normed, w_qkv, preferred_element_type=jnp.float32).astype(jnp.bfloat16)
    projected = projected.reshape(row_count, N_TENSOR, 3, group_heads, HEAD_DIM)
    queries = projected[:, :, 0].reshape(row_count, head_count, HEAD_DIM).astype(jnp.float32)
    keys_all = projected[:, :, 1].reshape(row_count, head_count, HEAD_DIM).astype(jnp.float32)
    values_all = projected[:, :, 2].reshape(row_count, head_count, HEAD_DIM).astype(jnp.float32)
    scores = jnp.einsum('qhd,khd->hqk', queries, keys_all) / math.sqrt(HEAD_DIM)
    same_image = segment[:, None] == segment[None, :]
    scores = jnp.where(same_image[None], scores, -1e+30)
    row_max = lax.optimization_barrier(jnp.max(scores, axis=-1, keepdims=True))
    exp_scores = jnp.exp(scores - row_max)
    weights = (exp_scores / lax.optimization_barrier(jnp.sum(exp_scores, axis=-1, keepdims=True))).astype(jnp.bfloat16)
    attended = jnp.einsum('hqk,khd->qhd', weights.astype(jnp.float32), values_all).astype(jnp.bfloat16)
    attended = attended.reshape(row_count, N_TENSOR, D // N_TENSOR)
    out_groups = w_out.reshape(N_TENSOR, D // N_TENSOR, D).astype(jnp.float32)
    attn_parts = jnp.einsum('rgc,gcd->grd', attended.astype(jnp.float32), out_groups).astype(jnp.bfloat16)
    attn_parts = lax.optimization_barrier(attn_parts)
    residual = (rows_here.astype(jnp.float32) + lax.optimization_barrier(jnp.sum(attn_parts.astype(jnp.float32), axis=0))).astype(jnp.bfloat16)
    normed_two = layer_norm(residual.astype(jnp.float32)).astype(jnp.bfloat16)
    hidden = jax.nn.gelu(jnp.dot(normed_two, w_fc1, preferred_element_type=jnp.float32), approximate=True).astype(jnp.bfloat16)
    hidden = hidden.reshape(row_count, N_TENSOR, FF // N_TENSOR)
    fc2_groups = w_fc2.reshape(N_TENSOR, FF // N_TENSOR, D).astype(jnp.float32)
    mlp_parts = jnp.einsum('rgc,gcd->grd', hidden.astype(jnp.float32), fc2_groups).astype(jnp.bfloat16)
    mlp_parts = lax.optimization_barrier(mlp_parts)
    layer_rows = (residual.astype(jnp.float32) + lax.optimization_barrier(jnp.sum(mlp_parts.astype(jnp.float32), axis=0))).astype(jnp.bfloat16)
    post_norm = layer_norm(layer_rows.astype(jnp.float32))
    member = (segment[None, :] == jnp.arange(IMG_DEV, dtype=jnp.int32)[:, None]).astype(jnp.float32)
    pooled = jnp.dot(member, post_norm, precision=lax.Precision.HIGHEST) / counts[:, None].astype(jnp.float32)
    return (layer_rows, pooled)

def reference(rows_in, patch_counts, row_slots, w_qkv, w_out, w_fc1, w_fc2, text_embeds, similarity_multiplier, similarity_shift_term):
    grouped = rows_in.reshape(N_DP, ROWS, D)
    worker = partial(one_device, w_qkv=w_qkv, w_out=w_out, w_fc1=w_fc1, w_fc2=w_fc2)
    layer_rows, pooled = lax.map(worker, (grouped, patch_counts))
    device_ids = jnp.arange(N_DP, dtype=jnp.int32)[:, None] * jnp.ones((1, ROWS), jnp.int32)
    placed = jnp.zeros((N_DP, ROWS, D), jnp.bfloat16).at[device_ids, row_slots].set(layer_rows)
    placed = placed.reshape(N_DP, N_DP, SLOT, D).transpose(1, 0, 2, 3)
    rows_out = placed.reshape(N_DP * ROWS, D)
    pooled = pooled.reshape(IMAGES, D)
    norm_img = jnp.sqrt(lax.optimization_barrier(jnp.sum(pooled * pooled, axis=1, keepdims=True)) + 1e-06)
    picture_unit_length_direction = pooled / norm_img
    text_f = text_embeds.astype(jnp.float32)
    caption_unit_length_direction = text_f / jnp.sqrt(lax.optimization_barrier(jnp.sum(text_f * text_f, axis=1, keepdims=True)) + 1e-06)
    similarity_sharpness_factor = similarity_multiplier[0]
    similarity_matrix_entries = similarity_sharpness_factor * jnp.dot(picture_unit_length_direction, caption_unit_length_direction.T, precision=lax.Precision.HIGHEST) + similarity_shift_term[0]
    similarity_matrix_derivative = jax.nn.sigmoid(similarity_matrix_entries) - jnp.eye(IMAGES, dtype=jnp.float32)
    picture_feature_derivative_wrt = similarity_sharpness_factor * jnp.dot(similarity_matrix_derivative, caption_unit_length_direction, precision=lax.Precision.HIGHEST)
    pooled_grad = (picture_feature_derivative_wrt - picture_unit_length_direction * lax.optimization_barrier(jnp.sum(picture_unit_length_direction * picture_feature_derivative_wrt, axis=1, keepdims=True))) / norm_img
    return (rows_out, pooled_grad)
```

```python
import math

import jax
import jax.numpy as jnp
from jax import lax
from jax.sharding import Mesh
from jax.sharding import PartitionSpec as P

HEAD_DIM = 72
N_YH, N_Z, N_X, N_YL, N_CORE = 2, 16, 4, 2, 2
DP = ("yh", "z", "x")
TP = ("yl", "core")
RING = ("yh", "z")
HIGH = lax.Precision.HIGHEST


def layer_norm(values):
    mean_val = jnp.mean(values, axis=-1, keepdims=True)
    centred = values - mean_val
    var_val = jnp.mean(centred * centred, axis=-1, keepdims=True)
    return centred * lax.rsqrt(var_val + 1e-06)


def unit_rows(values):
    return values / jnp.sqrt(jnp.sum(values * values, axis=1, keepdims=True) + 1e-06)


def swap_quarters(values):
    pairs = [(x * N_X + t, t * N_X + x) for x in range(N_X) for t in range(N_X)]
    return lax.ppermute(values, ("x",) + TP, pairs)


def sum_scatter(partial):
    rows, width = partial.shape
    parts = lax.all_to_all(partial.reshape(4, rows // 4, width), TP, 0, 0, tiled=True)
    return jnp.sum(parts.astype(jnp.float32), axis=0)


def per_device(rows_in, patch_counts, row_slots, w_qkv, w_out, w_fc1, w_fc2, text_embeds, multiplier, shift):
    row_count, width = rows_in.shape
    image_count = patch_counts.shape[1]
    head_count = w_out.shape[0] // HEAD_DIM
    quarter = row_count // 4
    ring = N_YH * N_Z
    my_x, my_t = lax.axis_index("x"), lax.axis_index(TP)

    slots = row_slots[0]
    peer, place = slots // 2, slots % 2
    order = (peer % N_X) * quarter + (peer // N_X) * 2 + place
    positions = jnp.arange(row_count, dtype=jnp.int32)
    moved = (positions[:, None] == order[None, :]).astype(jnp.bfloat16)
    bounds = jnp.cumsum(patch_counts[0])
    origin = jnp.sum(jnp.where(positions[:, None] == order[None, :], positions[None, :], 0), axis=1)
    segment = jnp.sum((origin[:, None] >= bounds[None, :]).astype(jnp.int32), axis=1)
    rows = jnp.dot(moved, rows_in, preferred_element_type=jnp.float32).astype(jnp.bfloat16)

    my_texts = swap_quarters(text_embeds)
    texts = lax.all_to_all(jnp.broadcast_to(my_texts[None], (ring,) + my_texts.shape), RING, 0, 0, tiled=True)
    texts = texts.reshape(ring * image_count, width)

    normed = layer_norm(rows.astype(jnp.float32)).astype(jnp.bfloat16)
    projected = jnp.dot(normed, w_qkv, preferred_element_type=jnp.float32).astype(jnp.bfloat16)
    projected = projected.reshape(row_count, 3, head_count, HEAD_DIM)
    queries, keys, values = projected[:, 0], projected[:, 1], projected[:, 2]
    scores = jnp.einsum("qhd,khd->hqk", queries, keys, preferred_element_type=jnp.float32) / math.sqrt(HEAD_DIM)
    same_image = segment[:, None] == segment[None, :]
    scores = jnp.where(same_image[None], scores, -1e30)
    row_max = jnp.max(scores, axis=-1, keepdims=True)
    exp_scores = jnp.exp(scores - row_max)
    weights = (exp_scores / jnp.sum(exp_scores, axis=-1, keepdims=True)).astype(jnp.bfloat16)
    attended = jnp.einsum("hqk,khd->qhd", weights, values, preferred_element_type=jnp.float32).astype(jnp.bfloat16)
    attended = attended.reshape(row_count, head_count * HEAD_DIM)
    attn_part = jnp.dot(attended, w_out, preferred_element_type=jnp.float32).astype(jnp.bfloat16)

    own = lax.dynamic_slice_in_dim(rows, my_t * quarter, quarter, axis=0)
    own_segment = lax.dynamic_slice_in_dim(segment, my_t * quarter, quarter, axis=0)
    resid = (own.astype(jnp.float32) + sum_scatter(attn_part)).astype(jnp.bfloat16)
    normed_own = layer_norm(resid.astype(jnp.float32)).astype(jnp.bfloat16)
    normed_two = lax.all_gather(normed_own, TP, axis=0, tiled=True)
    hidden = jax.nn.gelu(
        jnp.dot(normed_two, w_fc1, preferred_element_type=jnp.float32), approximate=True
    ).astype(jnp.bfloat16)
    mlp_part = jnp.dot(hidden, w_fc2, preferred_element_type=jnp.float32).astype(jnp.bfloat16)
    layer = (resid.astype(jnp.float32) + sum_scatter(mlp_part)).astype(jnp.bfloat16)

    outgoing = swap_quarters(layer).reshape(ring, 2, width)
    arrived = lax.all_to_all(outgoing, RING, 0, 0, tiled=True)
    arrived = lax.all_gather(arrived.reshape(quarter, width), TP, axis=0, tiled=True)
    rows_out = arrived.reshape(N_X, ring, 2, width).transpose(1, 0, 2, 3).reshape(row_count, width)

    images = jnp.arange(image_count, dtype=jnp.int32)
    member = (own_segment[None, :] == images[:, None]).astype(jnp.float32)
    pooled = jnp.dot(member, layer_norm(layer.astype(jnp.float32)), precision=HIGH)
    pooled = lax.psum(pooled, TP) / patch_counts[0][:, None].astype(jnp.float32)
    norm_img = jnp.sqrt(jnp.sum(pooled * pooled, axis=1, keepdims=True) + 1e-06)
    image_unit = pooled / norm_img
    text_unit = unit_rows(texts.astype(jnp.float32))
    logits = multiplier[0] * jnp.dot(image_unit, text_unit.T, precision=HIGH) + shift[0]
    text_peer = jnp.arange(ring, dtype=jnp.int32) * N_X + my_t
    text_index = (text_peer[:, None] * image_count + images[None, :]).reshape(-1)
    image_index = lax.axis_index(DP) * image_count + images
    target = (image_index[:, None] == text_index[None, :]).astype(jnp.float32)
    logit_grad = jax.nn.sigmoid(logits) - target
    image_grad = lax.psum(multiplier[0] * jnp.dot(logit_grad, text_unit, precision=HIGH), TP)
    along = jnp.sum(image_unit * image_grad, axis=1, keepdims=True)
    pooled_grad = (image_grad - image_unit * along) / norm_img
    return rows_out, pooled_grad


def solution(mesh):
    fine = Mesh(mesh.devices.reshape(N_YH, N_Z, N_X, N_YL, N_CORE), DP + TP)
    placed = (
        P(DP, None),
        P(DP, None),
        P(DP, None),
        P(None, TP),
        P(TP, None),
        P(None, TP),
        P(TP, None),
        P(DP, None),
        P(),
        P(),
    )
    return jax.shard_map(per_device, mesh=fine, in_specs=placed, out_specs=(P(DP, None), P(DP, None)), check_vma=False)
```

```python
import functools
import math

import jax
import jax.numpy as jnp
from jax import lax
from jax.experimental import pallas as pl
from jax.experimental.pallas import tpu as pltpu
from jax.sharding import Mesh
from jax.sharding import PartitionSpec as P

HEAD_DIM = 72
N_YH, N_Z, N_X, N_YL, N_CORE = 2, 16, 4, 2, 2
DP = ("yh", "z", "x")
TP = ("yl", "core")
RING = ("yh", "z")
HIGH = lax.Precision.HIGHEST
F32, BF16, I32 = jnp.float32, jnp.bfloat16, jnp.int32
VMEM = pl.BlockSpec(memory_space=pltpu.VMEM)
SMEM = pl.BlockSpec(memory_space=pltpu.SMEM)
CONTRACT_LAST = (((1,), (1,)), ((), ()))
CONTRACT_FIRST = (((0,), (0,)), ((), ()))
BIG = 28 * 2**20


def layer_norm(values):
    mean_val = jnp.mean(values, axis=-1, keepdims=True)
    centred = values - mean_val
    var_val = jnp.mean(centred * centred, axis=-1, keepdims=True)
    return centred * lax.rsqrt(var_val + 1e-06)


def unit_rows(values):
    return values / jnp.sqrt(jnp.sum(values * values, axis=1, keepdims=True) + 1e-06)


def swap_quarters(values, flip=0):
    pairs = [(x * N_X + t, (t ^ flip) * N_X + x) for x in range(N_X) for t in range(N_X)]
    return lax.ppermute(values, ("x",) + TP, pairs)


def attend_kernel(place, counts, slots, rows, w_qkv, w_out, keep, send, half, member, packed, part):
    n = rows.shape[0]
    core = place[0]
    slot = slots[...]
    peer = slot >> 1
    order = (peer & 1) * 128 + ((peer >> 1) & 1) * 64 + (peer >> 2) * 2 + (slot & 1)
    moved = jnp.where(lax.broadcasted_iota(I32, (n, n), 0) == order, 1.0, 0.0).astype(BF16)
    first, second = counts[0, 0], counts[0, 0] + counts[0, 1]

    def segment_of(position):
        return jnp.where(position >= first, 1.0, 0.0) + jnp.where(position >= second, 1.0, 0.0)

    seg_lanes = lax.dot_general(
        segment_of(lax.broadcasted_iota(I32, (8, n), 1)).astype(BF16), moved, CONTRACT_LAST, preferred_element_type=F32
    )
    seg_rows = jnp.dot(
        moved, segment_of(lax.broadcasted_iota(I32, (n, 128), 0)).astype(BF16), preferred_element_type=F32
    )
    same = seg_rows[:, :1] == seg_lanes[:1, :]
    ordered = jnp.dot(moved, rows[...], preferred_element_type=F32)
    packed[...] = ordered.astype(BF16)
    normed = layer_norm(ordered).astype(BF16)
    qkv = jnp.dot(normed, w_qkv[...], preferred_element_type=F32)
    heads = w_out.shape[0] // HEAD_DIM
    width = heads * HEAD_DIM
    outs = []
    for h in range(heads):
        q, k, v = (qkv[:, i * width + h * HEAD_DIM : i * width + (h + 1) * HEAD_DIM].astype(BF16) for i in range(3))
        scores = lax.dot_general(q, k, CONTRACT_LAST, preferred_element_type=F32) * (1.0 / math.sqrt(HEAD_DIM))
        scores = jnp.where(same, scores, -1e30)
        raised = jnp.exp(scores - jnp.max(scores, axis=-1, keepdims=True))
        total = jnp.sum(raised, axis=-1, keepdims=True)
        outs.append(jnp.dot(raised.astype(BF16), v, preferred_element_type=F32) / total)
    attended = jnp.concatenate(outs, axis=1).astype(BF16)
    part[...] = jnp.dot(attended, w_out[...], preferred_element_type=F32).astype(BF16)
    mine, other = pl.multiple_of(core * 128, 128), pl.multiple_of(128 - core * 128, 128)
    keep[...] = part[pl.ds(mine, 128), :]
    send[...] = part[pl.ds(other, 128), :]
    half[...] = packed[pl.ds(mine, 128), :]
    images = lax.broadcasted_iota(I32, (n, 128), 1).astype(F32)
    packed[:, :128] = jnp.where(seg_rows == images, 1.0, 0.0).astype(BF16)
    member[...] = packed[pl.ds(mine, 128), :128]


def mlp_kernel(place, half, own_sum, far_sum, member, w1a, w1b, w2a, w2b, first_out, second_out, resid, part):
    base = half[...].astype(F32) + own_sum[...].astype(F32) + far_sum[...].astype(F32)
    resid[...] = base.astype(BF16)
    normed = layer_norm(resid[...].astype(F32)).astype(BF16)
    total = None
    for w1, w2 in ((w1a, w2a), (w1b, w2b)):
        hidden = jax.nn.gelu(jnp.dot(normed, w1[...], preferred_element_type=F32), approximate=True).astype(BF16)
        piece = jnp.dot(hidden, w2[...], preferred_element_type=F32)
        total = piece if total is None else total + piece
    part[...] = total
    yl = place[1]
    mine, other = pl.multiple_of(yl * 64, 64), pl.multiple_of(64 - yl * 64, 64)
    width = half.shape[1]
    first_out[:, :width] = (part[pl.ds(mine, 64), :] + resid[pl.ds(mine, 64), :].astype(F32)).astype(BF16)
    first_out[:, width:] = member[pl.ds(mine, 64), :]
    second_out[...] = part[pl.ds(other, 64), :].astype(BF16)


def pool_kernel(first, second, pooled):
    width = second.shape[1]
    layer = (first[:, :width].astype(F32) + second[...].astype(F32)).astype(BF16)
    member = first[:, width:].astype(F32)
    full = lax.dot_general(
        member, layer_norm(layer.astype(F32)), CONTRACT_FIRST, precision=HIGH, preferred_element_type=F32
    )
    pooled[...] = full[:8]


def loss_kernel(image_base, text_base, counts, multiplier, shift, pooled_sum, texts, partial):
    row8 = lax.broadcasted_iota(I32, (8, 1), 0)
    count = jnp.where(row8 == 0, counts[0, 0], counts[0, 1]).astype(F32)
    pooled = pooled_sum[...] / count
    norm_img = jnp.sqrt(jnp.sum(pooled * pooled, axis=1, keepdims=True) + 1e-06)
    unit = pooled / norm_img
    text_unit = unit_rows(texts[...].astype(F32))
    logits = (
        multiplier[0] * lax.dot_general(unit, text_unit, CONTRACT_LAST, precision=HIGH, preferred_element_type=F32)
        + shift[0]
    )
    n_text = texts.shape[0]
    col = lax.broadcasted_iota(I32, (8, n_text), 1)
    text_index = (col >> 1) * (2 * N_X) + (col & 1) + text_base[0]
    image_index = lax.broadcasted_iota(I32, (8, n_text), 0) + image_base[0]
    slope = 1.0 / (1.0 + jnp.exp(-logits)) - jnp.where(text_index == image_index, 1.0, 0.0)
    grad = multiplier[0] * jnp.dot(slope, text_unit, precision=HIGH, preferred_element_type=F32)
    partial[...] = (grad - unit * jnp.sum(unit * grad, axis=1, keepdims=True)) / norm_img


def call(kernel, specs, outs, scratch=(), limit=None):
    many = isinstance(outs, list)
    return pl.pallas_call(
        kernel,
        in_specs=specs,
        out_specs=[VMEM] * len(outs) if many else VMEM,
        out_shape=outs,
        scratch_shapes=list(scratch),
        compiler_params=pltpu.CompilerParams(vmem_limit_bytes=limit),
    )


def per_device(rows_in, patch_counts, row_slots, w_qkv, w_out, w_fc1, w_fc2, text_embeds, multiplier, shift):
    row_count, width = rows_in.shape
    half_rows, quarter, ring = row_count // 2, row_count // 4, N_YH * N_Z
    shape = jax.ShapeDtypeStruct
    my_t, my_dp = lax.axis_index(TP), lax.axis_index(DP)
    place = jnp.stack([lax.axis_index("core"), lax.axis_index("yl")]).astype(I32)
    pair = [(0, 1), (1, 0)]

    my_texts = swap_quarters(text_embeds)

    keep, send, half, member = call(
        attend_kernel,
        [SMEM, SMEM, VMEM, VMEM, VMEM, VMEM],
        [
            shape((half_rows, width), BF16),
            shape((half_rows, width), BF16),
            shape((half_rows, width), BF16),
            shape((half_rows, 128), BF16),
        ],
        [pltpu.VMEM((row_count, width), BF16), pltpu.VMEM((row_count, width), BF16)],
        BIG,
    )(place, patch_counts, row_slots, rows_in, w_qkv, w_out)

    got = lax.ppermute(send, "core", pair)
    own_sum = (keep.astype(F32) + got.astype(F32)).astype(BF16)
    far_sum = lax.ppermute(own_sum, "yl", pair)
    w1b = lax.ppermute(w_fc1, "core", pair)
    w2b = lax.ppermute(w_fc2, "core", pair)
    spread = jnp.broadcast_to(my_texts[None], (ring,) + my_texts.shape)
    texts = lax.all_to_all(spread, RING, 0, 0, tiled=True).reshape(ring * 2, width)

    first, second = call(
        mlp_kernel,
        [SMEM] + [VMEM] * 8,
        [shape((quarter, width + 128), BF16), shape((quarter, width), BF16)],
        [pltpu.VMEM((half_rows, width), BF16), pltpu.VMEM((half_rows, width), F32)],
        BIG,
    )(place, half, own_sum, far_sum, member, w_fc1, w1b, w_fc2, w2b)

    first = swap_quarters(first)
    second = swap_quarters(second, 2)
    layer = (first[:, :width].astype(F32) + second.astype(F32)).astype(BF16)
    arrived = lax.all_to_all(layer.reshape(ring, 2, width), RING, 0, 0, tiled=True)
    rows_out = lax.all_gather(arrived, TP, axis=1, tiled=False).reshape(row_count, width)

    pooled = call(pool_kernel, [VMEM] * 2, shape((8, width), F32))(first, second)
    pooled = lax.psum(swap_quarters(pooled), TP)
    image_base = (my_dp * 2).astype(I32).reshape(1)
    text_base = (my_t * 2).astype(I32).reshape(1)
    partial = call(loss_kernel, [SMEM] * 5 + [VMEM] * 2, shape((8, width), F32))(
        image_base, text_base, patch_counts, multiplier, shift, pooled, texts
    )
    return rows_out, lax.psum(partial[:2], TP)


def solution(mesh):
    fine = Mesh(mesh.devices.reshape(N_YH, N_Z, N_X, N_YL, N_CORE), DP + TP)
    placed = (
        P(DP, None),
        P(DP, None),
        P(DP, None),
        P(None, TP),
        P(TP, None),
        P(None, TP),
        P(TP, None),
        P(DP, None),
        P(),
        P(),
    )
    return jax.shard_map(per_device, mesh=fine, in_specs=placed, out_specs=(P(DP, None), P(DP, None)), check_vma=False)
```

```python
import functools
import math

import jax
import jax.numpy as jnp
from jax import lax
from jax.experimental import pallas as pl
from jax.experimental.pallas import tpu as pltpu
from jax.sharding import Mesh
from jax.sharding import PartitionSpec as P

HEAD_DIM = 72
N_YH, N_Z, N_X, N_YL, N_CORE = 2, 16, 4, 2, 2
DP = ("yh", "z", "x")
TP = ("yl", "core")
RING = ("yh", "z")
HIGH = lax.Precision.HIGHEST
F32, BF16, I32 = jnp.float32, jnp.bfloat16, jnp.int32
VMEM = pl.BlockSpec(memory_space=pltpu.VMEM)
HBM = pl.BlockSpec(memory_space=pltpu.HBM)
SMEM = pl.BlockSpec(memory_space=pltpu.SMEM)
CONTRACT_LAST = (((1,), (1,)), ((), ()))
CONTRACT_FIRST = (((0,), (0,)), ((), ()))
BIG = 28 * 2**20


def layer_norm(values):
    mean_val = jnp.mean(values, axis=-1, keepdims=True)
    centred = values - mean_val
    var_val = jnp.mean(centred * centred, axis=-1, keepdims=True)
    return centred * lax.rsqrt(var_val + 1e-06)


def swap_quarters(values, flip=0):
    pairs = [(x * N_X + t, (t ^ flip) * N_X + x) for x in range(N_X) for t in range(N_X)]
    return lax.ppermute(values, ("x",) + TP, pairs)


def attend_kernel(
    place, counts, slots, rows_hbm, w_qkv_hbm, w_out_hbm, keep, send, half, member, packed, part, rows, w_qkv, w_out, sems
):
    fetches = [
        pltpu.make_async_copy(source, target, sems.at[i])
        for i, (source, target) in enumerate(((rows_hbm, rows), (w_qkv_hbm, w_qkv), (w_out_hbm, w_out)))
    ]
    for fetch in fetches:
        fetch.start()
    n = rows.shape[0]
    core = place[0]
    slot = slots[...]
    peer = slot >> 1
    order = (peer & 1) * 128 + ((peer >> 1) & 1) * 64 + (peer >> 2) * 2 + (slot & 1)
    moved = jnp.where(lax.broadcasted_iota(I32, (n, n), 0) == order, 1.0, 0.0).astype(BF16)
    first, second = counts[0, 0], counts[0, 0] + counts[0, 1]

    def segment_of(position):
        return jnp.where(position >= first, 1.0, 0.0) + jnp.where(position >= second, 1.0, 0.0)

    seg_lanes = lax.dot_general(
        segment_of(lax.broadcasted_iota(I32, (8, n), 1)).astype(BF16), moved, CONTRACT_LAST, preferred_element_type=F32
    )
    seg_rows = jnp.dot(
        moved, segment_of(lax.broadcasted_iota(I32, (n, 128), 0)).astype(BF16), preferred_element_type=F32
    )
    same = seg_rows[:, :1] == seg_lanes[:1, :]
    fetches[0].wait()
    ordered = jnp.dot(moved, rows[...], preferred_element_type=F32)
    packed[...] = ordered.astype(BF16)
    normed = layer_norm(ordered).astype(BF16)
    fetches[1].wait()
    qkv = lax.dot_general(normed, w_qkv[...], CONTRACT_LAST, preferred_element_type=F32)
    heads = w_out.shape[0] // HEAD_DIM
    width = heads * HEAD_DIM
    outs = []
    for h in range(heads):
        q, k, v = (qkv[:, i * width + h * HEAD_DIM : i * width + (h + 1) * HEAD_DIM].astype(BF16) for i in range(3))
        scores = lax.dot_general(q, k, CONTRACT_LAST, preferred_element_type=F32) * (1.0 / math.sqrt(HEAD_DIM))
        scores = jnp.where(same, scores, -1e30)
        raised = jnp.exp(scores - jnp.max(scores, axis=-1, keepdims=True))
        total = jnp.sum(raised, axis=-1, keepdims=True)
        outs.append(jnp.dot(raised.astype(BF16), v, preferred_element_type=F32) / total)
    attended = jnp.concatenate(outs, axis=1).astype(BF16)
    fetches[2].wait()
    part[...] = jnp.dot(attended, w_out[...], preferred_element_type=F32).astype(BF16)
    mine, other = pl.multiple_of(core * 128, 128), pl.multiple_of(128 - core * 128, 128)
    keep[...] = part[pl.ds(mine, 128), :]
    send[...] = part[pl.ds(other, 128), :]
    half[...] = packed[pl.ds(mine, 128), :]
    images = lax.broadcasted_iota(I32, (n, 128), 1).astype(F32)
    packed[:, :128] = jnp.where(seg_rows == images, 1.0, 0.0).astype(BF16)
    member[...] = packed[pl.ds(mine, 128), :128]


def mlp_kernel(
    place, half, own_sum, far_sum, member, text, w1a, w1b, w2a, w2b, first_out, second_out, share_out, resid, part
):
    base = half[...].astype(F32) + own_sum[...].astype(F32) + far_sum[...].astype(F32)
    resid[...] = base.astype(BF16)
    normed = layer_norm(resid[...].astype(F32)).astype(BF16)
    total = None
    for w1, w2 in ((w1a, w2a), (w1b, w2b)):
        hidden = lax.dot_general(normed, w1[...], CONTRACT_LAST, preferred_element_type=F32)
        hidden = jax.nn.gelu(hidden, approximate=True).astype(BF16)
        piece = jnp.dot(hidden, w2[...], preferred_element_type=F32)
        total = piece if total is None else total + piece
    part[...] = total
    share_out[...] = total.astype(BF16)
    yl = place[1]
    mine, other = pl.multiple_of(yl * 64, 64), pl.multiple_of(64 - yl * 64, 64)
    width = half.shape[1]
    first_out[:64, :width] = (part[pl.ds(mine, 64), :] + resid[pl.ds(mine, 64), :].astype(F32)).astype(BF16)
    first_out[64:, :width] = jnp.concatenate([text[...].astype(F32), jnp.zeros((14, width), F32)], axis=0).astype(BF16)
    second_out[...] = part[pl.ds(other, 64), :].astype(BF16)


def pool_kernel(resid, own_share, far_share, member, pooled):
    layer = resid[...].astype(F32) + own_share[...].astype(F32) + far_share[...].astype(F32)
    normed = layer_norm(layer.astype(BF16).astype(F32))
    high = normed.astype(BF16)
    low = (normed - high.astype(F32)).astype(BF16)
    full = lax.dot_general(member[...], high, CONTRACT_FIRST, preferred_element_type=F32)
    full += lax.dot_general(member[...], low, CONTRACT_FIRST, preferred_element_type=F32)
    pooled[...] = full[:8]


def two_parts(values):
    high = values.astype(BF16).astype(F32)
    return jnp.concatenate([high, values - high], axis=0).astype(BF16)


def loss_kernel(where, counts, multiplier, shift, pooled_sum, texts, grad_out):
    row8 = lax.broadcasted_iota(I32, (8, 1), 0)
    count = jnp.where(row8 == 0, counts[0, 0], counts[0, 1]).astype(F32)
    pooled = pooled_sum[...] / count
    norm_img = jnp.sqrt(jnp.sum(pooled * pooled, axis=1, keepdims=True) + 1e-06)
    unit = pooled / norm_img
    text = texts[...]
    square = text.astype(F32) * text.astype(F32)
    high = square.astype(BF16)
    low = (square - high.astype(F32)).astype(BF16)
    ones = jnp.ones((16, text.shape[1]), BF16)
    total = lax.dot_general(ones, high, CONTRACT_LAST, preferred_element_type=F32)
    total += lax.dot_general(ones, low, CONTRACT_LAST, preferred_element_type=F32)
    per_norm = lax.rsqrt(total[:8] + 1e-06)
    cosine = lax.dot_general(two_parts(unit), text, CONTRACT_LAST, preferred_element_type=F32)
    logits = multiplier[0] * (cosine[:8] + cosine[8:]) * per_norm + shift[0]
    column = lax.broadcasted_iota(I32, logits.shape, 1)
    text_index = (column >> 1) * (2 * N_X) + (column & 1) + where[1]
    image_index = lax.broadcasted_iota(I32, logits.shape, 0) + where[0]
    slope = 1.0 / (1.0 + jnp.exp(-logits)) - jnp.where(text_index == image_index, 1.0, 0.0)
    grad = jnp.dot(two_parts(slope * per_norm), text, preferred_element_type=F32)
    grad = multiplier[0] * (grad[:8] + grad[8:])
    grad_out[...] = ((grad - unit * jnp.sum(unit * grad, axis=1, keepdims=True)) / norm_img)[:2]


def call(kernel, specs, outs, scratch=(), limit=None, flops=10**7, nbytes=10**6):
    many = isinstance(outs, list)
    return pl.pallas_call(
        kernel,
        in_specs=specs,
        out_specs=[VMEM] * len(outs) if many else VMEM,
        out_shape=outs,
        scratch_shapes=list(scratch),
        compiler_params=pltpu.CompilerParams(vmem_limit_bytes=limit),
        cost_estimate=pl.CostEstimate(flops=flops, bytes_accessed=nbytes, transcendentals=0),
    )


def per_device(rows_in, patch_counts, row_slots, w_qkv, w_out, w_fc1, w_fc2, text_embeds, multiplier, shift):
    row_count, width = rows_in.shape
    half_rows, quarter, ring = row_count // 2, row_count // 4, N_YH * N_Z
    shape = jax.ShapeDtypeStruct
    place = jnp.stack([lax.axis_index("core"), lax.axis_index("yl")]).astype(I32)
    pair = [(0, 1), (1, 0)]

    keep, send, half, member = call(
        attend_kernel,
        [SMEM, SMEM, VMEM, HBM, HBM, HBM],
        [
            shape((half_rows, width), BF16),
            shape((half_rows, width), BF16),
            shape((half_rows, width), BF16),
            shape((half_rows, 128), BF16),
        ],
        [
            pltpu.VMEM((row_count, width), BF16),
            pltpu.VMEM((row_count, width), BF16),
            pltpu.VMEM((row_count, width), BF16),
            pltpu.VMEM((w_qkv.shape[1], width), BF16),
            pltpu.VMEM(w_out.shape, BF16),
            pltpu.SemaphoreType.DMA((3,)),
        ],
        BIG,
        2 * 10**9,
        8 * 10**6,
    )(place, patch_counts, row_slots, rows_in, w_qkv.T, w_out)

    got = lax.ppermute(send, "core", pair)
    own_sum = (keep.astype(F32) + got.astype(F32)).astype(BF16)
    own_sum, far_w1, far_w2 = lax.optimization_barrier((own_sum, w_fc1.T, w_fc2))
    far_sum = lax.ppermute(own_sum, "yl", pair)
    far_w1 = lax.ppermute(far_w1, "core", pair)
    far_w2 = lax.ppermute(far_w2, "core", pair)

    first, second, share, resid = call(
        mlp_kernel,
        [SMEM] + [VMEM] * 9,
        [
            shape((quarter + 16, width), BF16),
            shape((quarter, width), BF16),
            shape((half_rows, width), BF16),
            shape((half_rows, width), BF16),
        ],
        [pltpu.VMEM((half_rows, width), F32)],
        BIG,
        4 * 10**9,
        16 * 10**6,
    )(place, half, own_sum, far_sum, member, text_embeds, w_fc1.T, far_w1, w_fc2, far_w2)

    first = swap_quarters(first)
    second = swap_quarters(second, 2)
    far_share = lax.ppermute(share, "yl", pair)
    layer = (first[:quarter].astype(F32) + second.astype(F32)).astype(BF16).reshape(ring, 2, width)
    text = jnp.broadcast_to(first[quarter : quarter + 2][None], layer.shape)
    arrived = lax.all_to_all(jnp.concatenate([layer, text], axis=1), RING, 0, 0, tiled=True)

    pooled = call(pool_kernel, [VMEM] * 4, shape((8, width), F32))(resid, share, far_share, member)
    pooled = lax.psum(pooled, "core")
    where = jnp.stack([lax.axis_index(DP) * 2, lax.axis_index(TP) * 2]).astype(I32)
    grad = call(loss_kernel, [SMEM] * 4 + [VMEM] * 2, shape((2, width), F32))(
        where, patch_counts, multiplier, shift, pooled, arrived[:, 2:].reshape(quarter, width)
    )

    high = grad.astype(BF16)
    low = (grad - high.astype(F32)).astype(BF16)
    bundle = jnp.concatenate([arrived[:, :2], high[None], low[None]], axis=0)
    bundle = lax.all_gather(bundle, TP, axis=1, tiled=False)
    rows_out = bundle[:ring].reshape(row_count, width)
    return rows_out, jnp.sum(bundle[ring:].astype(F32), axis=(0, 1))


def solution(mesh):
    fine = Mesh(mesh.devices.reshape(N_YH, N_Z, N_X, N_YL, N_CORE), DP + TP)
    placed = (
        P(DP, None),
        P(DP, None),
        P(DP, None),
        P(None, TP),
        P(TP, None),
        P(None, TP),
        P(TP, None),
        P(DP, None),
        P(),
        P(),
    )
    return jax.shard_map(per_device, mesh=fine, in_specs=placed, out_specs=(P(DP, None), P(DP, None)), check_vma=False)
```

```python
import functools
import math

import jax
import jax.numpy as jnp
from jax import lax
from jax.experimental import pallas as pl
from jax.experimental.pallas import tpu as pltpu
from jax.sharding import Mesh
from jax.sharding import PartitionSpec as P

HEAD_DIM = 72
N_YH, N_Z, N_X, N_YL, N_CORE = 2, 16, 4, 2, 2
DP = ("yh", "z", "x")
TP = ("yl", "core")
RING = ("yh", "z")
HIGH = lax.Precision.HIGHEST
F32, BF16, I32 = jnp.float32, jnp.bfloat16, jnp.int32
VMEM = pl.BlockSpec(memory_space=pltpu.VMEM)
HBM = pl.BlockSpec(memory_space=pltpu.HBM)
SMEM = pl.BlockSpec(memory_space=pltpu.SMEM)
CONTRACT_LAST = (((1,), (1,)), ((), ()))
CONTRACT_FIRST = (((0,), (0,)), ((), ()))
BIG = 28 * 2**20
SMALL = 12 * 2**20
ATTEND_LIMIT = 61 * 2**20
NEAR_LIMIT = 40 * 2**20
NEAR_FLOPS = 50 * 10**9
ADD_FLOPS = 50 * 10**9
POOL_FLOPS = 50 * 10**9


def layer_norm(values):
    mean_val = jnp.mean(values, axis=-1, keepdims=True)
    centred = values - mean_val
    var_val = jnp.mean(centred * centred, axis=-1, keepdims=True)
    return centred * lax.rsqrt(var_val + 1e-06)


def swap_quarters(values, flip=0):
    pairs = [(x * N_X + t, (t ^ flip) * N_X + x) for x in range(N_X) for t in range(N_X)]
    return lax.ppermute(values, ("x",) + TP, pairs)


def attend_kernel(
    counts, slots, rows_hbm, w_qkv_hbm, w_out_hbm, keep, send, half, member, packed, part, rows, w_qkv, w_out, sems
):
    n, width = rows.shape[0], w_out.shape[0]
    thirds = [pl.ds(i * width, width) for i in range(3)]
    pieces = [(rows_hbm, rows)] + [(w_qkv_hbm.at[third], w_qkv.at[third]) for third in thirds] + [(w_out_hbm, w_out)]
    fetches = [pltpu.make_async_copy(source, target, sems.at[i]) for i, (source, target) in enumerate(pieces)]
    for fetch in fetches:
        fetch.start()
    core = lax.axis_index("core")
    slot = slots[...]
    peer = slot >> 1
    order = (peer & 1) * 128 + ((peer >> 1) & 1) * 64 + (peer >> 2) * 2 + (slot & 1)
    moved = jnp.where(lax.broadcasted_iota(I32, (n, n), 0) == order, 1.0, 0.0).astype(BF16)
    first, second = counts[:, 0:1], counts[:, 0:1] + counts[:, 1:2]

    def segment_of(position):
        return jnp.where(position >= first, 1.0, 0.0) + jnp.where(position >= second, 1.0, 0.0)

    seg_lanes = lax.dot_general(
        segment_of(lax.broadcasted_iota(I32, (8, n), 1)).astype(BF16), moved, CONTRACT_LAST, preferred_element_type=F32
    )
    seg_rows = jnp.dot(
        moved, segment_of(lax.broadcasted_iota(I32, (n, 128), 0)).astype(BF16), preferred_element_type=F32
    )
    same = seg_rows[:, :1] == seg_lanes[:1, :]
    fetches[0].wait()
    ordered = jnp.dot(moved, rows[...], preferred_element_type=F32)
    packed[...] = ordered.astype(BF16)
    normed = layer_norm(ordered).astype(BF16)
    qkv = []
    for i, third in enumerate(thirds):
        fetches[1 + i].wait()
        qkv.append(lax.dot_general(normed, w_qkv[third, :], CONTRACT_LAST, preferred_element_type=F32))
    outs = []
    for h in range(width // HEAD_DIM):
        q, k, v = (piece[:, h * HEAD_DIM : (h + 1) * HEAD_DIM].astype(BF16) for piece in qkv)
        scores = lax.dot_general(q, k, CONTRACT_LAST, preferred_element_type=F32) * (1.0 / math.sqrt(HEAD_DIM))
        scores = jnp.where(same, scores, -1e30)
        raised = jnp.exp(scores - jnp.max(scores, axis=-1, keepdims=True))
        total = jnp.sum(raised, axis=-1, keepdims=True)
        outs.append(jnp.dot(raised.astype(BF16), v, preferred_element_type=F32) / total)
    attended = jnp.concatenate(outs, axis=1).astype(BF16)
    fetches[4].wait()
    part[...] = jnp.dot(attended, w_out[...], preferred_element_type=F32).astype(BF16)
    mine, other = pl.multiple_of(core * 128, 128), pl.multiple_of(128 - core * 128, 128)
    keep[...] = part[pl.ds(mine, 128), :]
    send[...] = part[pl.ds(other, 128), :]
    half[...] = packed[pl.ds(mine, 128), :]
    images = lax.broadcasted_iota(I32, (n, 128), 1).astype(F32)
    packed[:, :128] = jnp.where(seg_rows == images, 1.0, 0.0).astype(BF16)
    member[...] = packed[pl.ds(mine, 128), :128]


def add_kernel(own, far, out):
    out[...] = (own[...].astype(F32) + far[...].astype(F32)).astype(BF16)


def mlp_share(normed, w1, w2):
    hidden = lax.dot_general(normed, w1, CONTRACT_LAST, preferred_element_type=F32)
    hidden = jax.nn.gelu(hidden, approximate=True).astype(BF16)
    return jnp.dot(hidden, w2, preferred_element_type=F32)


def near_kernel(half, own_sum, far_sum, w1_hbm, w2_hbm, resid, normed, part, w1, w2, sems):
    fetches = [
        pltpu.make_async_copy(source, target, sems.at[i])
        for i, (source, target) in enumerate(((w1_hbm, w1), (w2_hbm, w2)))
    ]
    for fetch in fetches:
        fetch.start()
    base = half[...].astype(F32) + own_sum[...].astype(F32) + far_sum[...].astype(F32)
    resid[...] = base.astype(BF16)
    normed[...] = layer_norm(resid[...].astype(F32)).astype(BF16)
    fetches[0].wait()
    hidden = lax.dot_general(normed[...], w1[...], CONTRACT_LAST, preferred_element_type=F32)
    hidden = jax.nn.gelu(hidden, approximate=True).astype(BF16)
    fetches[1].wait()
    part[...] = jnp.dot(hidden, w2[...], preferred_element_type=F32)


def far_kernel(resid, normed, part, text, w1, w2, first_out, second_out, share_out, total):
    total[...] = part[...] + mlp_share(normed[...], w1[...], w2[...])
    share_out[...] = total[...].astype(BF16)
    yl = lax.axis_index("yl")
    mine, other = pl.multiple_of(yl * 64, 64), pl.multiple_of(64 - yl * 64, 64)
    width = resid.shape[1]
    first_out[:64, :] = (total[pl.ds(mine, 64), :] + resid[pl.ds(mine, 64), :].astype(F32)).astype(BF16)
    first_out[64:, :] = jnp.concatenate([text[...].astype(F32), jnp.zeros((14, width), F32)], axis=0).astype(BF16)
    second_out[...] = total[pl.ds(other, 64), :].astype(BF16)


def pool_kernel(resid, own_share, far_share, member, pooled):
    layer = resid[...].astype(F32) + own_share[...].astype(F32) + far_share[...].astype(F32)
    normed = layer_norm(layer.astype(BF16).astype(F32))
    high = normed.astype(BF16)
    low = (normed - high.astype(F32)).astype(BF16)
    full = lax.dot_general(member[...], high, CONTRACT_FIRST, preferred_element_type=F32)
    full += lax.dot_general(member[...], low, CONTRACT_FIRST, preferred_element_type=F32)
    pooled[...] = full[:8]


def two_parts(values):
    high = values.astype(BF16).astype(F32)
    return jnp.concatenate([high, values - high], axis=0).astype(BF16)


def loss_kernel(where, counts, multiplier, shift, pooled_own, pooled_far, texts, grad_out):
    row8 = lax.broadcasted_iota(I32, (8, 1), 0)
    count = jnp.where(row8 == 0, counts[0, 0], counts[0, 1]).astype(F32)
    pooled = (pooled_own[...] + pooled_far[...]) / count
    norm_img = jnp.sqrt(jnp.sum(pooled * pooled, axis=1, keepdims=True) + 1e-06)
    unit = pooled / norm_img
    text = texts[...]
    square = text.astype(F32) * text.astype(F32)
    high = square.astype(BF16)
    low = (square - high.astype(F32)).astype(BF16)
    ones = jnp.ones((16, text.shape[1]), BF16)
    total = lax.dot_general(ones, high, CONTRACT_LAST, preferred_element_type=F32)
    total += lax.dot_general(ones, low, CONTRACT_LAST, preferred_element_type=F32)
    per_norm = lax.rsqrt(total[:8] + 1e-06)
    cosine = lax.dot_general(two_parts(unit), text, CONTRACT_LAST, preferred_element_type=F32)
    logits = multiplier[0] * (cosine[:8] + cosine[8:]) * per_norm + shift[0]
    column = lax.broadcasted_iota(I32, logits.shape, 1)
    text_index = (column >> 1) * (2 * N_X) + (column & 1) + where[1]
    image_index = lax.broadcasted_iota(I32, logits.shape, 0) + where[0]
    slope = 1.0 / (1.0 + jnp.exp(-logits)) - jnp.where(text_index == image_index, 1.0, 0.0)
    grad = jnp.dot(two_parts(slope * per_norm), text, preferred_element_type=F32)
    grad = multiplier[0] * (grad[:8] + grad[8:])
    grad_out[...] = ((grad - unit * jnp.sum(unit * grad, axis=1, keepdims=True)) / norm_img)[:2].astype(BF16)


def call(kernel, specs, outs, scratch=(), limit=None, flops=10**7, nbytes=10**6):
    many = isinstance(outs, list)
    return pl.pallas_call(
        kernel,
        in_specs=specs,
        out_specs=[VMEM] * len(outs) if many else VMEM,
        out_shape=outs,
        scratch_shapes=list(scratch),
        compiler_params=pltpu.CompilerParams(vmem_limit_bytes=limit),
        cost_estimate=pl.CostEstimate(flops=flops, bytes_accessed=nbytes, transcendentals=0),
    )


def per_device(rows_in, patch_counts, row_slots, w_qkv, w_out, w_fc1, w_fc2, text_embeds, multiplier, shift):
    row_count, width = rows_in.shape
    half_rows, quarter, ring = row_count // 2, row_count // 4, N_YH * N_Z
    shape = jax.ShapeDtypeStruct
    pair = [(0, 1), (1, 0)]

    keep, send, half, member = call(
        attend_kernel,
        [VMEM, VMEM, HBM, HBM, HBM],
        [
            shape((half_rows, width), BF16),
            shape((half_rows, width), BF16),
            shape((half_rows, width), BF16),
            shape((half_rows, 128), BF16),
        ],
        [
            pltpu.VMEM((row_count, width), BF16),
            pltpu.VMEM((row_count, width), BF16),
            pltpu.VMEM((row_count, width), BF16),
            pltpu.VMEM((w_qkv.shape[1], width), BF16),
            pltpu.VMEM(w_out.shape, BF16),
            pltpu.SemaphoreType.DMA((5,)),
        ],
        ATTEND_LIMIT,
        2 * 10**9,
        8 * 10**6,
    )(patch_counts, row_slots, rows_in, w_qkv.T, w_out)

    got = lax.ppermute(send, "core", pair)
    own_sum = call(add_kernel, [VMEM] * 2, shape((half_rows, width), BF16), limit=SMALL, flops=ADD_FLOPS)(keep, got)
    own_sum, far_w1, far_w2 = lax.optimization_barrier((own_sum, w_fc1.T, w_fc2))
    far_sum = lax.ppermute(own_sum, "yl", pair)
    far_w1 = lax.ppermute(far_w1, "core", pair)
    far_w2 = lax.ppermute(far_w2, "core", pair)

    hidden = w_fc2.shape[0]
    resid, normed, part = call(
        near_kernel,
        [VMEM, VMEM, VMEM, HBM, HBM],
        [shape((half_rows, width), BF16), shape((half_rows, width), BF16), shape((half_rows, width), F32)],
        [pltpu.VMEM((hidden, width), BF16), pltpu.VMEM((hidden, width), BF16), pltpu.SemaphoreType.DMA((2,))],
        NEAR_LIMIT,
        NEAR_FLOPS,
        16 * 10**6,
    )(half, own_sum, far_sum, w_fc1.T, w_fc2)
    first, second, share = call(
        far_kernel,
        [VMEM] * 6,
        [shape((quarter + 16, width), BF16), shape((quarter, width), BF16), shape((half_rows, width), BF16)],
        [pltpu.VMEM((half_rows, width), F32)],
        BIG,
        4 * 10**9,
        16 * 10**6,
    )(resid, normed, part, text_embeds, far_w1, far_w2)

    first = swap_quarters(first)
    second = swap_quarters(second, 2)
    far_share = lax.ppermute(share, "yl", pair)
    layer = (first[:quarter].astype(F32) + second.astype(F32)).astype(BF16).reshape(ring, 2, width)
    text = jnp.broadcast_to(first[quarter : quarter + 2][None], layer.shape)
    arrived = lax.all_to_all(jnp.concatenate([layer, text], axis=1), RING, 0, 0, tiled=True)

    pooled = call(pool_kernel, [VMEM] * 4, shape((8, width), F32), limit=SMALL, flops=POOL_FLOPS)(resid, share, far_share, member)
    pooled_far = lax.ppermute(pooled, "core", pair)
    where = jnp.stack([lax.axis_index(DP) * 2, lax.axis_index(TP) * 2]).astype(I32)
    grad = call(loss_kernel, [SMEM] * 4 + [VMEM] * 3, shape((2, width), BF16), limit=SMALL)(
        where, patch_counts, multiplier, shift, pooled, pooled_far, arrived[:, 2:].reshape(quarter, width)
    )

    bundle = jnp.concatenate([arrived[:, :2], grad[None]], axis=0)
    bundle = lax.all_gather(bundle, TP, axis=1, tiled=False)
    rows_out = bundle[:ring].reshape(row_count, width)
    return rows_out, jnp.sum(bundle[ring].astype(F32), axis=0)


def solution(mesh):
    fine = Mesh(mesh.devices.reshape(N_YH, N_Z, N_X, N_YL, N_CORE), DP + TP)
    placed = (
        P(DP, None),
        P(DP, None),
        P(DP, None),
        P(None, TP),
        P(TP, None),
        P(None, TP),
        P(TP, None),
        P(DP, None),
        P(),
        P(),
    )
    return jax.shard_map(per_device, mesh=fine, in_specs=placed, out_specs=(P(DP, None), P(DP, None)), check_vma=False)
```

```python
import functools
import math

import jax
import jax.numpy as jnp
from jax import lax
from jax.experimental import pallas as pl
from jax.experimental.pallas import tpu as pltpu
from jax.sharding import Mesh
from jax.sharding import PartitionSpec as P

HEAD_DIM = 72
N_YH, N_Z, N_XH, N_XL, N_YL, N_CORE = 2, 16, 2, 2, 2, 2
DP = ("yh", "z", "xh", "xl")
TP = ("yl", "core")
QUARTER = ("yh", "xh")
RING = ("z", "xl")
HIGH = lax.Precision.HIGHEST
F32, BF16, I32 = jnp.float32, jnp.bfloat16, jnp.int32
VMEM = pl.BlockSpec(memory_space=pltpu.VMEM)
HBM = pl.BlockSpec(memory_space=pltpu.HBM)
SMEM = pl.BlockSpec(memory_space=pltpu.SMEM)
CONTRACT_LAST = (((1,), (1,)), ((), ()))
CONTRACT_FIRST = (((0,), (0,)), ((), ()))
BIG = 28 * 2**20
SMALL = 12 * 2**20
ATTEND_LIMIT = 28 * 2**20
NEAR_LIMIT = 28 * 2**20
NEAR_FLOPS = 50 * 10**9
ADD_FLOPS = 500 * 10**9
POOL_FLOPS = 50 * 10**9


def layer_norm(values):
    mean_val = jnp.mean(values, axis=-1, keepdims=True)
    centred = values - mean_val
    var_val = jnp.mean(centred * centred, axis=-1, keepdims=True)
    return centred * lax.rsqrt(var_val + 1e-06)


def swap_quarters(values, flip=0):
    pairs = [(q * 4 + t, (t ^ flip) * 4 + q) for q in range(4) for t in range(4)]
    return lax.ppermute(values, QUARTER + TP, pairs)


def attend_kernel(
    counts, slots, rows_hbm, w_qkv_hbm, w_out_hbm, keep, send, half, member, packed, part, rows, w_qkv, w_out, sems
):
    n, width = rows.shape[0], w_out.shape[0]
    thirds = [pl.ds(i * width, width) for i in range(3)]
    pieces = [(rows_hbm, rows)] + [(w_qkv_hbm.at[third], w_qkv.at[third]) for third in thirds] + [(w_out_hbm, w_out)]
    fetches = [pltpu.make_async_copy(source, target, sems.at[i]) for i, (source, target) in enumerate(pieces)]
    for fetch in fetches:
        fetch.start()
    core = lax.axis_index("core")
    slot = slots[...]
    peer = slot >> 1
    order = ((peer >> 1) & 1) * 128 + (peer >> 6) * 64 + ((peer >> 2) & 15) * 4 + (peer & 1) * 2 + (slot & 1)
    moved = jnp.where(lax.broadcasted_iota(I32, (n, n), 0) == order, 1.0, 0.0).astype(BF16)
    first, second = counts[:, 0:1], counts[:, 0:1] + counts[:, 1:2]

    def segment_of(position):
        return jnp.where(position >= first, 1.0, 0.0) + jnp.where(position >= second, 1.0, 0.0)

    seg_lanes = lax.dot_general(
        segment_of(lax.broadcasted_iota(I32, (8, n), 1)).astype(BF16), moved, CONTRACT_LAST, preferred_element_type=F32
    )
    seg_rows = jnp.dot(
        moved, segment_of(lax.broadcasted_iota(I32, (n, 128), 0)).astype(BF16), preferred_element_type=F32
    )
    same = seg_rows[:, :1] == seg_lanes[:1, :]
    fetches[0].wait()
    ordered = jnp.dot(moved, rows[...], preferred_element_type=F32)
    packed[...] = ordered.astype(BF16)
    normed = layer_norm(ordered).astype(BF16)
    qkv = []
    for i, third in enumerate(thirds):
        fetches[1 + i].wait()
        qkv.append(lax.dot_general(normed, w_qkv[third, :], CONTRACT_LAST, preferred_element_type=F32))
    outs = []
    for h in range(width // HEAD_DIM):
        q, k, v = (piece[:, h * HEAD_DIM : (h + 1) * HEAD_DIM].astype(BF16) for piece in qkv)
        scores = lax.dot_general(q, k, CONTRACT_LAST, preferred_element_type=F32) * (1.0 / math.sqrt(HEAD_DIM))
        scores = jnp.where(same, scores, -1e30)
        raised = jnp.exp(scores - jnp.max(scores, axis=-1, keepdims=True))
        total = jnp.sum(raised, axis=-1, keepdims=True)
        outs.append(jnp.dot(raised.astype(BF16), v, preferred_element_type=F32) / total)
    attended = jnp.concatenate(outs, axis=1).astype(BF16)
    fetches[4].wait()
    part[...] = jnp.dot(attended, w_out[...], preferred_element_type=F32).astype(BF16)
    mine, other = pl.multiple_of(core * 128, 128), pl.multiple_of(128 - core * 128, 128)
    keep[...] = part[pl.ds(mine, 128), :]
    send[...] = part[pl.ds(other, 128), :]
    half[...] = packed[pl.ds(mine, 128), :]
    images = lax.broadcasted_iota(I32, (n, 128), 1).astype(F32)
    packed[:, :128] = jnp.where(seg_rows == images, 1.0, 0.0).astype(BF16)
    member[...] = packed[pl.ds(mine, 128), :128]


def add_kernel(own, far, out):
    out[...] = (own[...].astype(F32) + far[...].astype(F32)).astype(BF16)


def mlp_share(normed, w1, w2):
    hidden = lax.dot_general(normed, w1, CONTRACT_LAST, preferred_element_type=F32)
    hidden = jax.nn.gelu(hidden, approximate=True).astype(BF16)
    return jnp.dot(hidden, w2, preferred_element_type=F32)


def near_kernel(half, own_sum, far_sum, w1, w2, resid, normed, part):
    base = half[...].astype(F32) + own_sum[...].astype(F32) + far_sum[...].astype(F32)
    resid[...] = base.astype(BF16)
    normed[...] = layer_norm(resid[...].astype(F32)).astype(BF16)
    part[...] = mlp_share(normed[...], w1[...], w2[...])


def far_kernel(resid, normed, part, text, w1, w2, first_out, second_out, share_out, total):
    total[...] = part[...] + mlp_share(normed[...], w1[...], w2[...])
    share_out[...] = total[...].astype(BF16)
    yl = lax.axis_index("yl")
    mine, other = pl.multiple_of(yl * 64, 64), pl.multiple_of(64 - yl * 64, 64)
    width = resid.shape[1]
    first_out[:64, :] = (total[pl.ds(mine, 64), :] + resid[pl.ds(mine, 64), :].astype(F32)).astype(BF16)
    first_out[64:, :] = jnp.concatenate([text[...].astype(F32), jnp.zeros((14, width), F32)], axis=0).astype(BF16)
    second_out[...] = total[pl.ds(other, 64), :].astype(BF16)


def pool_kernel(resid, own_share, far_share, member, pooled):
    layer = resid[...].astype(F32) + own_share[...].astype(F32) + far_share[...].astype(F32)
    normed = layer_norm(layer.astype(BF16).astype(F32))
    high = normed.astype(BF16)
    low = (normed - high.astype(F32)).astype(BF16)
    full = lax.dot_general(member[...], high, CONTRACT_FIRST, preferred_element_type=F32)
    full += lax.dot_general(member[...], low, CONTRACT_FIRST, preferred_element_type=F32)
    pooled[...] = full[:8]


def two_parts(values):
    high = values.astype(BF16).astype(F32)
    return jnp.concatenate([high, values - high], axis=0).astype(BF16)


def loss_kernel(where, counts, multiplier, shift, pooled_own, pooled_far, texts, grad_out):
    row8 = lax.broadcasted_iota(I32, (8, 1), 0)
    count = jnp.where(row8 == 0, counts[0, 0], counts[0, 1]).astype(F32)
    pooled = (pooled_own[...] + pooled_far[...]) / count
    norm_img = jnp.sqrt(jnp.sum(pooled * pooled, axis=1, keepdims=True) + 1e-06)
    unit = pooled / norm_img
    text = texts[...]
    square = text.astype(F32) * text.astype(F32)
    high = square.astype(BF16)
    low = (square - high.astype(F32)).astype(BF16)
    ones = jnp.ones((16, text.shape[1]), BF16)
    total = lax.dot_general(ones, high, CONTRACT_LAST, preferred_element_type=F32)
    total += lax.dot_general(ones, low, CONTRACT_LAST, preferred_element_type=F32)
    per_norm = lax.rsqrt(total[:8] + 1e-06)
    cosine = lax.dot_general(two_parts(unit), text, CONTRACT_LAST, preferred_element_type=F32)
    logits = multiplier[0] * (cosine[:8] + cosine[8:]) * per_norm + shift[0]
    column = lax.broadcasted_iota(I32, logits.shape, 1)
    text_index = (column >> 2) * (4 * N_XH) + (column & 3) + where[1]
    image_index = lax.broadcasted_iota(I32, logits.shape, 0) + where[0]
    slope = 1.0 / (1.0 + jnp.exp(-logits)) - jnp.where(text_index == image_index, 1.0, 0.0)
    grad = jnp.dot(two_parts(slope * per_norm), text, preferred_element_type=F32)
    grad = multiplier[0] * (grad[:8] + grad[8:])
    grad_out[...] = ((grad - unit * jnp.sum(unit * grad, axis=1, keepdims=True)) / norm_img)[:2].astype(BF16)


def call(kernel, specs, outs, scratch=(), limit=None, flops=10**7, nbytes=10**6):
    many = isinstance(outs, list)
    return pl.pallas_call(
        kernel,
        in_specs=specs,
        out_specs=[VMEM] * len(outs) if many else VMEM,
        out_shape=outs,
        scratch_shapes=list(scratch),
        compiler_params=pltpu.CompilerParams(vmem_limit_bytes=limit),
        cost_estimate=pl.CostEstimate(flops=flops, bytes_accessed=nbytes, transcendentals=0),
    )


def per_device(rows_in, patch_counts, row_slots, w_qkv, w_out, w_fc1, w_fc2, text_embeds, multiplier, shift):
    row_count, width = rows_in.shape
    half_rows, quarter, ring = row_count // 2, row_count // 4, N_Z * N_XL
    shape = jax.ShapeDtypeStruct
    pair = [(0, 1), (1, 0)]

    keep, send, half, member = call(
        attend_kernel,
        [VMEM, VMEM, HBM, HBM, HBM],
        [
            pltpu.VMEM((half_rows, width), BF16),
            pltpu.VMEM((half_rows, width), BF16),
            pltpu.VMEM((half_rows, width), BF16),
            pltpu.VMEM((half_rows, 128), BF16),
        ],
        [
            pltpu.VMEM((row_count, width), BF16),
            pltpu.VMEM((row_count, width), BF16),
            pltpu.VMEM((row_count, width), BF16),
            pltpu.VMEM((w_qkv.shape[1], width), BF16),
            pltpu.VMEM(w_out.shape, BF16),
            pltpu.SemaphoreType.DMA((5,)),
        ],
        ATTEND_LIMIT,
        2 * 10**9,
        8 * 10**6,
    )(*(pltpu.with_memory_space_constraint(x, pltpu.HBM) for x in (patch_counts, row_slots, rows_in, w_qkv.T, w_out)))

    got = lax.ppermute(send, "core", pair)
    own_sum = call(add_kernel, [VMEM] * 2, shape((half_rows, width), BF16), limit=SMALL, flops=ADD_FLOPS)(keep, got)
    own_sum, far_w1, far_w2 = lax.optimization_barrier((own_sum, w_fc1.T, w_fc2))
    far_sum = lax.ppermute(own_sum, "yl", pair)
    far_w1 = lax.ppermute(far_w1, "core", pair)
    far_w2 = lax.ppermute(far_w2, "core", pair)

    resid, normed, part = call(
        near_kernel,
        [VMEM] * 5,
        [shape((half_rows, width), BF16), shape((half_rows, width), BF16), shape((half_rows, width), F32)],
        (),
        NEAR_LIMIT,
        NEAR_FLOPS,
        16 * 10**6,
    )(half, own_sum, far_sum, w_fc1.T, w_fc2)
    first, second, share = call(
        far_kernel,
        [VMEM] * 6,
        [shape((quarter + 16, width), BF16), shape((quarter, width), BF16), shape((half_rows, width), BF16)],
        [pltpu.VMEM((half_rows, width), F32)],
        BIG,
        4 * 10**9,
        16 * 10**6,
    )(resid, normed, part, text_embeds, far_w1, far_w2)

    first = swap_quarters(first)
    second = swap_quarters(second, 2)
    far_share = lax.ppermute(share, "yl", pair)
    layer = (first[:quarter].astype(F32) + second.astype(F32)).astype(BF16).reshape(ring, 2, width)
    text = jnp.broadcast_to(first[quarter : quarter + 2][None], layer.shape)
    arrived = lax.all_to_all(jnp.concatenate([layer, text], axis=1), RING, 0, 0, tiled=True)

    pooled = call(pool_kernel, [VMEM] * 4, shape((8, width), F32), limit=SMALL, flops=POOL_FLOPS)(resid, share, far_share, member)
    pooled_far = lax.ppermute(pooled, "core", pair)
    where = jnp.stack([lax.axis_index(DP) * 2, lax.axis_index("yl") * 128 + lax.axis_index("core") * 4]).astype(I32)
    grad = call(loss_kernel, [SMEM] * 4 + [VMEM] * 3, shape((2, width), BF16), limit=SMALL)(
        where, patch_counts, multiplier, shift, pooled, pooled_far, arrived[:, 2:].reshape(quarter, width)
    )

    bundle = jnp.concatenate([arrived[:, :2], grad[None]], axis=0)
    bundle = lax.all_gather(bundle, TP, axis=1, tiled=False)
    rows_out = bundle[:ring].reshape(N_Z, N_XL, N_YH, N_XH, 2, width).transpose(2, 0, 3, 1, 4, 5).reshape(row_count, width)
    return rows_out, jnp.sum(bundle[ring].astype(F32), axis=0)


def solution(mesh):
    fine = Mesh(mesh.devices.reshape(N_YH, N_Z, N_XH, N_XL, N_YL, N_CORE), DP + TP)
    placed = (
        P(DP, None),
        P(DP, None),
        P(DP, None),
        P(None, TP),
        P(TP, None),
        P(None, TP),
        P(TP, None),
        P(DP, None),
        P(),
        P(),
    )
    return jax.shard_map(per_device, mesh=fine, in_specs=placed, out_specs=(P(DP, None), P(DP, None)), check_vma=False)
```

```python
import functools
import math

import jax
import jax.numpy as jnp
from jax import lax
from jax.experimental import pallas as pl
from jax.experimental.pallas import tpu as pltpu
from jax.sharding import Mesh
from jax.sharding import PartitionSpec as P

HEAD_DIM = 72
N_YH, N_Z, N_XH, N_XL, N_YL, N_CORE = 2, 16, 2, 2, 2, 2
DP = ("yh", "z", "xh", "xl")
TP = ("yl", "core")
QUARTER = ("yh", "xh")
RING = ("z", "xl")
HIGH = lax.Precision.HIGHEST
F32, BF16, I32 = jnp.float32, jnp.bfloat16, jnp.int32
VMEM = pl.BlockSpec(memory_space=pltpu.VMEM)
HBM = pl.BlockSpec(memory_space=pltpu.HBM)
SMEM = pl.BlockSpec(memory_space=pltpu.SMEM)
CONTRACT_LAST = (((1,), (1,)), ((), ()))
CONTRACT_FIRST = (((0,), (0,)), ((), ()))
BIG = 28 * 2**20
SMALL = 12 * 2**20
ATTEND_LIMIT = 28 * 2**20
NEAR_LIMIT = 28 * 2**20
NEAR_FLOPS = 50 * 10**9
ADD_FLOPS = 500 * 10**9
POOL_FLOPS = 50 * 10**9


def layer_norm(values):
    mean_val = jnp.mean(values, axis=-1, keepdims=True)
    centred = values - mean_val
    var_val = jnp.mean(centred * centred, axis=-1, keepdims=True)
    return centred * lax.rsqrt(var_val + 1e-06)


def swap_quarters(values, flip=0):
    pairs = [(q * 4 + t, (t ^ flip) * 4 + q) for q in range(4) for t in range(4)]
    return lax.ppermute(values, QUARTER + TP, pairs)


def attend_kernel(
    counts, slots, rows_hbm, w_qkv_hbm, w_out_hbm, keep, send, half, member, packed, part, rows, w_qkv, w_out, sems
):
    n, width = rows.shape[0], w_out.shape[0]
    thirds = [pl.ds(i * width, width) for i in range(3)]
    pieces = [(rows_hbm, rows)] + [(w_qkv_hbm.at[third], w_qkv.at[third]) for third in thirds] + [(w_out_hbm, w_out)]
    fetches = [pltpu.make_async_copy(source, target, sems.at[i]) for i, (source, target) in enumerate(pieces)]
    for fetch in fetches:
        fetch.start()
    core = lax.axis_index("core")
    slot = slots[...]
    peer = slot >> 1
    order = ((peer >> 1) & 1) * 128 + (peer >> 6) * 64 + ((peer >> 2) & 15) * 4 + (peer & 1) * 2 + (slot & 1)
    moved = jnp.where(lax.broadcasted_iota(I32, (n, n), 0) == order, 1.0, 0.0).astype(BF16)
    first, second = counts[:, 0:1], counts[:, 0:1] + counts[:, 1:2]

    def segment_of(position):
        return jnp.where(position >= first, 1.0, 0.0) + jnp.where(position >= second, 1.0, 0.0)

    seg_lanes = lax.dot_general(
        segment_of(lax.broadcasted_iota(I32, (8, n), 1)).astype(BF16), moved, CONTRACT_LAST, preferred_element_type=F32
    )
    seg_rows = jnp.dot(
        moved, segment_of(lax.broadcasted_iota(I32, (n, 128), 0)).astype(BF16), preferred_element_type=F32
    )
    same = seg_rows[:, :1] == seg_lanes[:1, :]
    fetches[0].wait()
    ordered = jnp.dot(moved, rows[...], preferred_element_type=F32)
    packed[...] = ordered.astype(BF16)
    normed = layer_norm(ordered).astype(BF16)
    for i in range(3):
        fetches[1 + i].wait()
    qkv = lax.dot_general(normed, w_qkv[...], CONTRACT_LAST, preferred_element_type=F32)
    qkv = [qkv[:, i * width : (i + 1) * width] for i in range(3)]
    outs = []
    for h in range(width // HEAD_DIM):
        q, k, v = (piece[:, h * HEAD_DIM : (h + 1) * HEAD_DIM].astype(BF16) for piece in qkv)
        scores = lax.dot_general(q, k, CONTRACT_LAST, preferred_element_type=F32) * (1.0 / math.sqrt(HEAD_DIM))
        scores = jnp.where(same, scores, -1e30)
        raised = jnp.exp(scores - jnp.max(scores, axis=-1, keepdims=True))
        total = jnp.sum(raised, axis=-1, keepdims=True)
        outs.append(jnp.dot(raised.astype(BF16), v, preferred_element_type=F32) / total)
    attended = jnp.concatenate(outs, axis=1).astype(BF16)
    fetches[4].wait()
    part[...] = jnp.dot(attended, w_out[...], preferred_element_type=F32).astype(BF16)
    mine, other = pl.multiple_of(core * 128, 128), pl.multiple_of(128 - core * 128, 128)
    keep[...] = part[pl.ds(mine, 128), :]
    send[...] = part[pl.ds(other, 128), :]
    half[...] = packed[pl.ds(mine, 128), :]
    images = lax.broadcasted_iota(I32, (n, 128), 1).astype(F32)
    packed[:, :128] = jnp.where(seg_rows == images, 1.0, 0.0).astype(BF16)
    member[...] = packed[pl.ds(mine, 128), :128]


def add_kernel(own, far, out):
    out[...] = (own[...].astype(F32) + far[...].astype(F32)).astype(BF16)


def mlp_share(normed, w1, w2):
    hidden = lax.dot_general(normed, w1, CONTRACT_LAST, preferred_element_type=F32)
    hidden = jax.nn.gelu(hidden, approximate=True).astype(BF16)
    return jnp.dot(hidden, w2, preferred_element_type=F32)


def near_kernel(half, own_sum, far_sum, w1, w2, resid, normed, part):
    base = half[...].astype(F32) + own_sum[...].astype(F32) + far_sum[...].astype(F32)
    resid[...] = base.astype(BF16)
    normed[...] = layer_norm(resid[...].astype(F32)).astype(BF16)
    part[...] = mlp_share(normed[...], w1[...], w2[...])


def far_kernel(resid, normed, part, text, w1, w2, first_out, second_out, share_out, total):
    total[...] = part[...] + mlp_share(normed[...], w1[...], w2[...])
    share_out[...] = total[...].astype(BF16)
    yl = lax.axis_index("yl")
    mine, other = pl.multiple_of(yl * 64, 64), pl.multiple_of(64 - yl * 64, 64)
    width = resid.shape[1]
    first_out[:64, :] = (total[pl.ds(mine, 64), :] + resid[pl.ds(mine, 64), :].astype(F32)).astype(BF16)
    first_out[64:, :] = jnp.concatenate([text[...].astype(F32), jnp.zeros((14, width), F32)], axis=0).astype(BF16)
    second_out[...] = total[pl.ds(other, 64), :].astype(BF16)


def pool_kernel(resid, own_share, far_share, member, pooled):
    layer = resid[...].astype(F32) + own_share[...].astype(F32) + far_share[...].astype(F32)
    normed = layer_norm(layer.astype(BF16).astype(F32))
    high = normed.astype(BF16)
    low = (normed - high.astype(F32)).astype(BF16)
    full = lax.dot_general(member[...], high, CONTRACT_FIRST, preferred_element_type=F32)
    full += lax.dot_general(member[...], low, CONTRACT_FIRST, preferred_element_type=F32)
    pooled[...] = full[:8]


def two_parts(values):
    high = values.astype(BF16).astype(F32)
    return jnp.concatenate([high, values - high], axis=0).astype(BF16)


def loss_kernel(where, counts, multiplier, shift, pooled_own, pooled_far, texts, grad_out):
    row8 = lax.broadcasted_iota(I32, (8, 1), 0)
    count = jnp.where(row8 == 0, counts[0, 0], counts[0, 1]).astype(F32)
    pooled = (pooled_own[...] + pooled_far[...]) / count
    norm_img = jnp.sqrt(jnp.sum(pooled * pooled, axis=1, keepdims=True) + 1e-06)
    unit = pooled / norm_img
    text = texts[...]
    square = text.astype(F32) * text.astype(F32)
    high = square.astype(BF16)
    low = (square - high.astype(F32)).astype(BF16)
    ones = jnp.ones((16, text.shape[1]), BF16)
    total = lax.dot_general(ones, high, CONTRACT_LAST, preferred_element_type=F32)
    total += lax.dot_general(ones, low, CONTRACT_LAST, preferred_element_type=F32)
    per_norm = lax.rsqrt(total[:8] + 1e-06)
    cosine = lax.dot_general(two_parts(unit), text, CONTRACT_LAST, preferred_element_type=F32)
    logits = multiplier[0] * (cosine[:8] + cosine[8:]) * per_norm + shift[0]
    column = lax.broadcasted_iota(I32, logits.shape, 1)
    text_index = (column >> 2) * (4 * N_XH) + (column & 3) + where[1]
    image_index = lax.broadcasted_iota(I32, logits.shape, 0) + where[0]
    slope = 1.0 / (1.0 + jnp.exp(-logits)) - jnp.where(text_index == image_index, 1.0, 0.0)
    grad = jnp.dot(two_parts(slope * per_norm), text, preferred_element_type=F32)
    grad = multiplier[0] * (grad[:8] + grad[8:])
    grad_out[...] = ((grad - unit * jnp.sum(unit * grad, axis=1, keepdims=True)) / norm_img)[:2].astype(BF16)


def place_kernel(gathered, rows_out, grad_out):
    planes, count, _ = gathered.shape
    per_half = planes // N_YH
    row = lax.broadcasted_iota(I32, (128, count), 0)
    column = lax.broadcasted_iota(I32, (128, count), 1)
    last = jnp.where(lax.broadcasted_iota(I32, (16, count), 1) == count - 1, 1.0, 0.0).astype(BF16)
    grads = [None] * 2
    for half in range(N_YH):
        total = None
        for k in range(per_half):
            plane = gathered[half * per_half + k]
            xh, image = k // 2, k % 2
            target = (column >> 1) * 8 + xh * 4 + (column & 1) * 2 + image
            pick = jnp.where((row == target) & (column < count - 1), 1.0, 0.0).astype(BF16)
            piece = jnp.dot(pick, plane, preferred_element_type=F32)
            total = piece if total is None else total + piece
            share = jnp.dot(last, plane, preferred_element_type=F32)[:1]
            grads[image] = share if grads[image] is None else grads[image] + share
        rows_out[half * 128 : (half + 1) * 128, :] = total.astype(BF16)
    grad_out[...] = jnp.concatenate(grads, axis=0)


def call(kernel, specs, outs, scratch=(), limit=None, flops=10**7, nbytes=10**6):
    many = isinstance(outs, list)
    return pl.pallas_call(
        kernel,
        in_specs=specs,
        out_specs=[VMEM] * len(outs) if many else VMEM,
        out_shape=outs,
        scratch_shapes=list(scratch),
        compiler_params=pltpu.CompilerParams(vmem_limit_bytes=limit),
        cost_estimate=pl.CostEstimate(flops=flops, bytes_accessed=nbytes, transcendentals=0),
    )


def per_device(rows_in, patch_counts, row_slots, w_qkv, w_out, w_fc1, w_fc2, text_embeds, multiplier, shift):
    row_count, width = rows_in.shape
    half_rows, quarter, ring = row_count // 2, row_count // 4, N_Z * N_XL
    shape = jax.ShapeDtypeStruct
    pair = [(0, 1), (1, 0)]

    keep, send, half, member = call(
        attend_kernel,
        [VMEM, VMEM, HBM, HBM, HBM],
        [
            pltpu.VMEM((half_rows, width), BF16),
            pltpu.VMEM((half_rows, width), BF16),
            pltpu.VMEM((half_rows, width), BF16),
            pltpu.VMEM((half_rows, 128), BF16),
        ],
        [
            pltpu.VMEM((row_count, width), BF16),
            pltpu.VMEM((row_count, width), BF16),
            pltpu.VMEM((row_count, width), BF16),
            pltpu.VMEM((w_qkv.shape[1], width), BF16),
            pltpu.VMEM(w_out.shape, BF16),
            pltpu.SemaphoreType.DMA((5,)),
        ],
        ATTEND_LIMIT,
        2 * 10**9,
        8 * 10**6,
    )(*(pltpu.with_memory_space_constraint(x, pltpu.HBM) for x in (patch_counts, row_slots, rows_in, w_qkv.T, w_out)))

    got = lax.ppermute(send, "core", pair)
    own_sum = call(add_kernel, [VMEM] * 2, shape((half_rows, width), BF16), limit=SMALL, flops=ADD_FLOPS)(keep, got)
    own_sum, far_w1, far_w2 = lax.optimization_barrier((own_sum, w_fc1.T, w_fc2))
    far_sum = lax.ppermute(own_sum, "yl", pair)
    far_w1 = lax.ppermute(far_w1, "core", pair)
    far_w2 = lax.ppermute(far_w2, "core", pair)

    resid, normed, part = call(
        near_kernel,
        [VMEM] * 5,
        [shape((half_rows, width), BF16), shape((half_rows, width), BF16), shape((half_rows, width), F32)],
        (),
        NEAR_LIMIT,
        NEAR_FLOPS,
        16 * 10**6,
    )(half, own_sum, far_sum, w_fc1.T, w_fc2)
    first, second, share = call(
        far_kernel,
        [VMEM] * 6,
        [shape((quarter + 16, width), BF16), shape((quarter, width), BF16), shape((half_rows, width), BF16)],
        [pltpu.VMEM((half_rows, width), F32)],
        BIG,
        4 * 10**9,
        16 * 10**6,
    )(resid, normed, part, text_embeds, far_w1, far_w2)

    first = swap_quarters(first)
    second = swap_quarters(second, 2)
    far_share = lax.ppermute(share, "yl", pair)
    layer = (first[:quarter].astype(F32) + second.astype(F32)).astype(BF16).reshape(ring, 2, width)
    text = jnp.broadcast_to(first[quarter : quarter + 2][None], layer.shape)
    arrived = lax.all_to_all(jnp.concatenate([layer, text], axis=1), RING, 0, 0, tiled=True)

    pooled = call(pool_kernel, [VMEM] * 4, shape((8, width), F32), limit=SMALL, flops=POOL_FLOPS)(resid, share, far_share, member)
    pooled_far = lax.ppermute(pooled, "core", pair)
    where = jnp.stack([lax.axis_index(DP) * 2, lax.axis_index("yl") * 128 + lax.axis_index("core") * 4]).astype(I32)
    grad = call(loss_kernel, [SMEM] * 4 + [VMEM] * 3, shape((2, width), BF16), limit=SMALL)(
        where, patch_counts, multiplier, shift, pooled, pooled_far, arrived[:, 2:].reshape(quarter, width)
    )

    bundle = jnp.concatenate([arrived[:, :2], grad[None]], axis=0)
    bundle = lax.all_gather(bundle, TP, axis=1, tiled=False)
    gathered = bundle.reshape(ring + 1, 8, width).transpose(1, 0, 2)
    return call(place_kernel, [VMEM], [shape((row_count, width), BF16), shape((2, width), F32)], limit=SMALL)(gathered)


def solution(mesh):
    fine = Mesh(mesh.devices.reshape(N_YH, N_Z, N_XH, N_XL, N_YL, N_CORE), DP + TP)
    placed = (
        P(DP, None),
        P(DP, None),
        P(DP, None),
        P(None, TP),
        P(TP, None),
        P(None, TP),
        P(TP, None),
        P(DP, None),
        P(),
        P(),
    )
    return jax.shard_map(per_device, mesh=fine, in_specs=placed, out_specs=(P(DP, None), P(DP, None)), check_vma=False)
```

```python
import functools
import math

import jax
import jax.numpy as jnp
from jax import lax
from jax.experimental import pallas as pl
from jax.experimental.pallas import tpu as pltpu
from jax.sharding import Mesh
from jax.sharding import PartitionSpec as P

HEAD_DIM = 72
N_YH, N_Z, N_XH, N_XL, N_YL, N_CORE = 2, 16, 2, 2, 2, 2
DP = ("yh", "z", "xh", "xl")
TP = ("yl", "core")
QUARTER = ("yh", "xh")
RING = ("z", "xl")
HIGH = lax.Precision.HIGHEST
F32, BF16, I32 = jnp.float32, jnp.bfloat16, jnp.int32
VMEM = pl.BlockSpec(memory_space=pltpu.VMEM)
HBM = pl.BlockSpec(memory_space=pltpu.HBM)
SMEM = pl.BlockSpec(memory_space=pltpu.SMEM)
CONTRACT_LAST = (((1,), (1,)), ((), ()))
CONTRACT_FIRST = (((0,), (0,)), ((), ()))
BIG = 28 * 2**20
SMALL = 12 * 2**20
ATTEND_LIMIT = 28 * 2**20
NEAR_LIMIT = 28 * 2**20
NEAR_FLOPS = 50 * 10**9
ADD_FLOPS = 500 * 10**9
POOL_FLOPS = 50 * 10**9


def layer_norm(values):
    mean_val = jnp.mean(values, axis=-1, keepdims=True)
    centred = values - mean_val
    var_val = jnp.mean(centred * centred, axis=-1, keepdims=True)
    return centred * lax.rsqrt(var_val + 1e-06)


def swap_quarters(values, flip=0):
    pairs = [(q * 4 + t, (t ^ flip) * 4 + q) for q in range(4) for t in range(4)]
    return lax.ppermute(values, QUARTER + TP, pairs)


def attend_kernel(
    counts, slots, rows_hbm, w_qkv_hbm, w_out_hbm, keep, send, half, member, packed, part, rows, w_qkv, w_out, sems
):
    n, width = rows.shape[0], w_out.shape[0]
    thirds = [pl.ds(i * width, width) for i in range(3)]
    pieces = [(rows_hbm, rows)] + [(w_qkv_hbm.at[third], w_qkv.at[third]) for third in thirds] + [(w_out_hbm, w_out)]
    fetches = [pltpu.make_async_copy(source, target, sems.at[i]) for i, (source, target) in enumerate(pieces)]
    for fetch in fetches:
        fetch.start()
    core = lax.axis_index("core")
    slot = slots[...]
    peer = slot >> 1
    order = ((peer >> 1) & 1) * 128 + (peer >> 6) * 64 + ((peer >> 2) & 15) * 4 + (peer & 1) * 2 + (slot & 1)
    moved = jnp.where(lax.broadcasted_iota(I32, (n, n), 0) == order, 1.0, 0.0).astype(BF16)
    first, second = counts[:, 0:1], counts[:, 0:1] + counts[:, 1:2]

    def segment_of(position):
        return jnp.where(position >= first, 1.0, 0.0) + jnp.where(position >= second, 1.0, 0.0)

    seg_lanes = lax.dot_general(
        segment_of(lax.broadcasted_iota(I32, (8, n), 1)).astype(BF16), moved, CONTRACT_LAST, preferred_element_type=F32
    )
    seg_rows = jnp.dot(
        moved, segment_of(lax.broadcasted_iota(I32, (n, 128), 0)).astype(BF16), preferred_element_type=F32
    )
    same = seg_rows[:, :1] == seg_lanes[:1, :]
    fetches[0].wait()
    ordered = jnp.dot(moved, rows[...], preferred_element_type=F32)
    packed[...] = ordered.astype(BF16)
    normed = layer_norm(ordered).astype(BF16)
    for i in range(3):
        fetches[1 + i].wait()
    qkv = lax.dot_general(normed, w_qkv[...], CONTRACT_LAST, preferred_element_type=F32)
    qkv = [qkv[:, i * width : (i + 1) * width] for i in range(3)]
    outs = []
    for h in range(width // HEAD_DIM):
        q, k, v = (piece[:, h * HEAD_DIM : (h + 1) * HEAD_DIM].astype(BF16) for piece in qkv)
        scores = lax.dot_general(q, k, CONTRACT_LAST, preferred_element_type=F32) * (1.0 / math.sqrt(HEAD_DIM))
        scores = jnp.where(same, scores, -1e30)
        raised = jnp.exp(scores - jnp.max(scores, axis=-1, keepdims=True))
        total = jnp.sum(raised, axis=-1, keepdims=True)
        outs.append(jnp.dot(raised.astype(BF16), v, preferred_element_type=F32) / total)
    attended = jnp.concatenate(outs, axis=1).astype(BF16)
    fetches[4].wait()
    part[...] = jnp.dot(attended, w_out[...], preferred_element_type=F32).astype(BF16)
    mine, other = pl.multiple_of(core * 128, 128), pl.multiple_of(128 - core * 128, 128)
    keep[...] = part[pl.ds(mine, 128), :]
    send[...] = part[pl.ds(other, 128), :]
    half[...] = packed[pl.ds(mine, 128), :]
    images = lax.broadcasted_iota(I32, (n, 128), 1).astype(F32)
    packed[:, :128] = jnp.where(seg_rows == images, 1.0, 0.0).astype(BF16)
    member[...] = packed[pl.ds(mine, 128), :128]


def add_kernel(own, far, out):
    out[...] = (own[...].astype(F32) + far[...].astype(F32)).astype(BF16)


def mlp_share(normed, w1, w2):
    hidden = lax.dot_general(normed, w1, CONTRACT_LAST, preferred_element_type=F32)
    hidden = jax.nn.gelu(hidden, approximate=True).astype(BF16)
    return jnp.dot(hidden, w2, preferred_element_type=F32)


def near_kernel(half, own_sum, far_sum, w1, w2, resid, normed, part):
    base = half[...].astype(F32) + own_sum[...].astype(F32) + far_sum[...].astype(F32)
    resid[...] = base.astype(BF16)
    normed[...] = layer_norm(resid[...].astype(F32)).astype(BF16)
    part[...] = mlp_share(normed[...], w1[...], w2[...])


def far_kernel(resid, normed, part, text, w1, w2, first_out, second_out, share_out, total):
    total[...] = part[...] + mlp_share(normed[...], w1[...], w2[...])
    share_out[...] = total[...].astype(BF16)
    yl = lax.axis_index("yl")
    mine, other = pl.multiple_of(yl * 64, 64), pl.multiple_of(64 - yl * 64, 64)
    width = resid.shape[1]
    first_out[:64, :] = (total[pl.ds(mine, 64), :] + resid[pl.ds(mine, 64), :].astype(F32)).astype(BF16)
    first_out[64:, :] = jnp.concatenate([text[...].astype(F32), jnp.zeros((14, width), F32)], axis=0).astype(BF16)
    second_out[...] = total[pl.ds(other, 64), :].astype(BF16)


def pool_kernel(resid, own_share, far_share, member, pooled):
    layer = resid[...].astype(F32) + own_share[...].astype(F32) + far_share[...].astype(F32)
    normed = layer_norm(layer.astype(BF16).astype(F32))
    high = normed.astype(BF16)
    low = (normed - high.astype(F32)).astype(BF16)
    full = lax.dot_general(member[...], high, CONTRACT_FIRST, preferred_element_type=F32)
    full += lax.dot_general(member[...], low, CONTRACT_FIRST, preferred_element_type=F32)
    pooled[...] = full[:8]


def two_parts(values):
    high = values.astype(BF16).astype(F32)
    return jnp.concatenate([high, values - high], axis=0).astype(BF16)


def loss_kernel(where, counts, multiplier, shift, pooled_own, pooled_far, texts, grad_out):
    row8 = lax.broadcasted_iota(I32, (8, 1), 0)
    count = jnp.where(row8 == 0, counts[0, 0], counts[0, 1]).astype(F32)
    pooled = (pooled_own[...] + pooled_far[...]) / count
    norm_img = jnp.sqrt(jnp.sum(pooled * pooled, axis=1, keepdims=True) + 1e-06)
    unit = pooled / norm_img
    text = texts[...]
    square = text.astype(F32) * text.astype(F32)
    high = square.astype(BF16)
    low = (square - high.astype(F32)).astype(BF16)
    ones = jnp.ones((16, text.shape[1]), BF16)
    total = lax.dot_general(ones, high, CONTRACT_LAST, preferred_element_type=F32)
    total += lax.dot_general(ones, low, CONTRACT_LAST, preferred_element_type=F32)
    per_norm = lax.rsqrt(total[:8] + 1e-06)
    cosine = lax.dot_general(two_parts(unit), text, CONTRACT_LAST, preferred_element_type=F32)
    logits = multiplier[0] * (cosine[:8] + cosine[8:]) * per_norm + shift[0]
    column = lax.broadcasted_iota(I32, logits.shape, 1)
    text_index = (column >> 2) * (4 * N_XH) + (column & 3) + where[1]
    image_index = lax.broadcasted_iota(I32, logits.shape, 0) + where[0]
    slope = 1.0 / (1.0 + jnp.exp(-logits)) - jnp.where(text_index == image_index, 1.0, 0.0)
    grad = jnp.dot(two_parts(slope * per_norm), text, preferred_element_type=F32)
    grad = multiplier[0] * (grad[:8] + grad[8:])
    grad_out[...] = ((grad - unit * jnp.sum(unit * grad, axis=1, keepdims=True)) / norm_img)[:2].astype(BF16)


def place_kernel(gathered, rows_out, grad_out):
    planes, count, width = gathered.shape
    per_half, ring = planes // N_YH, count - 1
    row = lax.broadcasted_iota(I32, (128, 128), 0)
    column = lax.broadcasted_iota(I32, (128, 128), 1)
    plane, member = column // ring, column % ring
    target = (member >> 1) * 8 + (plane >> 1) * 4 + (member & 1) * 2 + (plane & 1)
    pick = jnp.where(row == target, 1.0, 0.0).astype(BF16)
    is_share = lax.broadcasted_iota(I32, (count, width), 0) == ring
    shares = [jnp.zeros((count, width), F32) for _ in range(2)]
    for half in range(N_YH):
        mine = [gathered[half * per_half + k] for k in range(per_half)]
        ordered = jnp.dot(pick, jnp.concatenate([p[:ring] for p in mine], axis=0), preferred_element_type=F32)
        rows_out[half * 128 : (half + 1) * 128, :] = ordered.astype(BF16)
        for k in range(per_half):
            shares[k % 2] += mine[k].astype(F32)
    grads = [jnp.sum(jnp.where(is_share, share, 0.0), axis=0, keepdims=True) for share in shares]
    grad_out[...] = jnp.concatenate(grads, axis=0)


def call(kernel, specs, outs, scratch=(), limit=None, flops=10**7, nbytes=10**6):
    many = isinstance(outs, list)
    return pl.pallas_call(
        kernel,
        in_specs=specs,
        out_specs=[VMEM] * len(outs) if many else VMEM,
        out_shape=outs,
        scratch_shapes=list(scratch),
        compiler_params=pltpu.CompilerParams(vmem_limit_bytes=limit),
        cost_estimate=pl.CostEstimate(flops=flops, bytes_accessed=nbytes, transcendentals=0),
    )


def per_device(rows_in, patch_counts, row_slots, w_qkv, w_out, w_fc1, w_fc2, text_embeds, multiplier, shift):
    row_count, width = rows_in.shape
    half_rows, quarter, ring = row_count // 2, row_count // 4, N_Z * N_XL
    shape = jax.ShapeDtypeStruct
    pair = [(0, 1), (1, 0)]

    keep, send, half, member = call(
        attend_kernel,
        [VMEM, VMEM, HBM, HBM, HBM],
        [
            pltpu.VMEM((half_rows, width), BF16),
            pltpu.VMEM((half_rows, width), BF16),
            pltpu.VMEM((half_rows, width), BF16),
            pltpu.VMEM((half_rows, 128), BF16),
        ],
        [
            pltpu.VMEM((row_count, width), BF16),
            pltpu.VMEM((row_count, width), BF16),
            pltpu.VMEM((row_count, width), BF16),
            pltpu.VMEM((w_qkv.shape[1], width), BF16),
            pltpu.VMEM(w_out.shape, BF16),
            pltpu.SemaphoreType.DMA((5,)),
        ],
        ATTEND_LIMIT,
        2 * 10**9,
        8 * 10**6,
    )(*(pltpu.with_memory_space_constraint(x, pltpu.HBM) for x in (patch_counts, row_slots, rows_in, w_qkv.T, w_out)))

    got = lax.ppermute(send, "core", pair)
    own_sum = call(add_kernel, [VMEM] * 2, shape((half_rows, width), BF16), limit=SMALL, flops=ADD_FLOPS)(keep, got)
    own_sum, far_w1, far_w2 = lax.optimization_barrier((own_sum, w_fc1.T, w_fc2))
    far_sum = lax.ppermute(own_sum, "yl", pair)
    far_w1 = lax.ppermute(far_w1, "core", pair)
    far_w2 = lax.ppermute(far_w2, "core", pair)

    resid, normed, part = call(
        near_kernel,
        [VMEM] * 5,
        [shape((half_rows, width), BF16), shape((half_rows, width), BF16), shape((half_rows, width), F32)],
        (),
        NEAR_LIMIT,
        NEAR_FLOPS,
        16 * 10**6,
    )(half, own_sum, far_sum, w_fc1.T, w_fc2)
    first, second, share = call(
        far_kernel,
        [VMEM] * 6,
        [shape((quarter + 16, width), BF16), shape((quarter, width), BF16), shape((half_rows, width), BF16)],
        [pltpu.VMEM((half_rows, width), F32)],
        BIG,
        4 * 10**9,
        16 * 10**6,
    )(resid, normed, part, text_embeds, far_w1, far_w2)

    first = swap_quarters(first)
    second = swap_quarters(second, 2)
    far_share = lax.ppermute(share, "yl", pair)
    layer = (first[:quarter].astype(F32) + second.astype(F32)).astype(BF16).reshape(ring, 2, width)
    text = jnp.broadcast_to(first[quarter : quarter + 2][None], layer.shape)
    arrived = lax.all_to_all(jnp.concatenate([layer, text], axis=1), RING, 0, 0, tiled=True)

    pooled = call(pool_kernel, [VMEM] * 4, shape((8, width), F32), limit=SMALL, flops=POOL_FLOPS)(resid, share, far_share, member)
    pooled_far = lax.ppermute(pooled, "core", pair)
    where = jnp.stack([lax.axis_index(DP) * 2, lax.axis_index("yl") * 128 + lax.axis_index("core") * 4]).astype(I32)
    grad = call(loss_kernel, [SMEM] * 4 + [VMEM] * 3, shape((2, width), BF16), limit=SMALL)(
        where, patch_counts, multiplier, shift, pooled, pooled_far, arrived[:, 2:].reshape(quarter, width)
    )

    bundle = jnp.concatenate([arrived[:, :2], grad[None]], axis=0)
    bundle = lax.all_gather(bundle, TP, axis=1, tiled=False)
    gathered = bundle.reshape(ring + 1, 8, width).transpose(1, 0, 2)
    return call(place_kernel, [VMEM], [shape((row_count, width), BF16), shape((2, width), F32)], limit=SMALL)(gathered)


def solution(mesh):
    fine = Mesh(mesh.devices.reshape(N_YH, N_Z, N_XH, N_XL, N_YL, N_CORE), DP + TP)
    placed = (
        P(DP, None),
        P(DP, None),
        P(DP, None),
        P(None, TP),
        P(TP, None),
        P(None, TP),
        P(TP, None),
        P(DP, None),
        P(),
        P(),
    )
    return jax.shard_map(per_device, mesh=fine, in_specs=placed, out_specs=(P(DP, None), P(DP, None)), check_vma=False)
```

```python
import functools
import math

import jax
import jax.numpy as jnp
from jax import lax
from jax.experimental import pallas as pl
from jax.experimental.pallas import tpu as pltpu
from jax.sharding import Mesh
from jax.sharding import PartitionSpec as P

HEAD_DIM = 72
N_YH, N_Z, N_XH, N_XL, N_YL, N_CORE = 2, 16, 2, 2, 2, 2
DP = ("yh", "z", "xh", "xl")
TP = ("yl", "core")
QUARTER = ("yh", "xh")
RING = ("z", "xl")
HIGH = lax.Precision.HIGHEST
F32, BF16, I32 = jnp.float32, jnp.bfloat16, jnp.int32
VMEM = pl.BlockSpec(memory_space=pltpu.VMEM)
HBM = pl.BlockSpec(memory_space=pltpu.HBM)
SMEM = pl.BlockSpec(memory_space=pltpu.SMEM)
CONTRACT_LAST = (((1,), (1,)), ((), ()))
CONTRACT_FIRST = (((0,), (0,)), ((), ()))
BIG = 28 * 2**20
SMALL = 12 * 2**20
ATTEND_LIMIT = 28 * 2**20
NEAR_LIMIT = 28 * 2**20
NEAR_FLOPS = 50 * 10**9
ADD_FLOPS = 500 * 10**9
POOL_FLOPS = 50 * 10**9


def layer_norm(values):
    mean_val = jnp.mean(values, axis=-1, keepdims=True)
    centred = values - mean_val
    var_val = jnp.mean(centred * centred, axis=-1, keepdims=True)
    return centred * lax.rsqrt(var_val + 1e-06)


def swap_quarters(values, flip=0):
    pairs = [(q * 4 + t, (t ^ flip) * 4 + q) for q in range(4) for t in range(4)]
    return lax.ppermute(values, QUARTER + TP, pairs)


def attend_kernel(
    counts, slots, rows_hbm, w_qkv_hbm, w_out_hbm, send, kept, half, member, packed, attended, rows, w_qkv, w_out, sems
):
    n, width = rows.shape[0], w_out.shape[0]
    thirds = [pl.ds(i * width, width) for i in range(3)]
    pieces = [(rows_hbm, rows)] + [(w_qkv_hbm.at[third], w_qkv.at[third]) for third in thirds] + [(w_out_hbm, w_out)]
    fetches = [pltpu.make_async_copy(source, target, sems.at[i]) for i, (source, target) in enumerate(pieces)]
    for fetch in fetches:
        fetch.start()
    core = lax.axis_index("core")
    slot = slots[...]
    peer = slot >> 1
    order = ((peer >> 1) & 1) * 128 + (peer >> 6) * 64 + ((peer >> 2) & 15) * 4 + (peer & 1) * 2 + (slot & 1)
    moved = jnp.where(lax.broadcasted_iota(I32, (n, n), 0) == order, 1.0, 0.0).astype(BF16)
    first, second = counts[:, 0:1], counts[:, 0:1] + counts[:, 1:2]

    def segment_of(position):
        return jnp.where(position >= first, 1.0, 0.0) + jnp.where(position >= second, 1.0, 0.0)

    seg_lanes = lax.dot_general(
        segment_of(lax.broadcasted_iota(I32, (8, n), 1)).astype(BF16), moved, CONTRACT_LAST, preferred_element_type=F32
    )
    seg_rows = jnp.dot(
        moved, segment_of(lax.broadcasted_iota(I32, (n, 128), 0)).astype(BF16), preferred_element_type=F32
    )
    same = seg_rows[:, :1] == seg_lanes[:1, :]
    fetches[0].wait()
    ordered = jnp.dot(moved, rows[...], preferred_element_type=F32)
    packed[...] = ordered.astype(BF16)
    normed = layer_norm(ordered).astype(BF16)
    for i in range(3):
        fetches[1 + i].wait()
    qkv = lax.dot_general(normed, w_qkv[...], CONTRACT_LAST, preferred_element_type=F32)
    qkv = [qkv[:, i * width : (i + 1) * width] for i in range(3)]
    outs = []
    for h in range(width // HEAD_DIM):
        q, k, v = (piece[:, h * HEAD_DIM : (h + 1) * HEAD_DIM].astype(BF16) for piece in qkv)
        scores = lax.dot_general(q, k, CONTRACT_LAST, preferred_element_type=F32) * (1.0 / math.sqrt(HEAD_DIM))
        scores = jnp.where(same, scores, -1e30)
        raised = jnp.exp(scores - jnp.max(scores, axis=-1, keepdims=True))
        total = jnp.sum(raised, axis=-1, keepdims=True)
        outs.append(jnp.dot(raised.astype(BF16), v, preferred_element_type=F32) / total)
    attended[...] = jnp.concatenate(outs, axis=1).astype(BF16)
    mine, other = pl.multiple_of(core * 128, 128), pl.multiple_of(128 - core * 128, 128)
    kept[...] = attended[pl.ds(mine, 128), :]
    fetches[4].wait()
    send[...] = jnp.dot(attended[pl.ds(other, 128), :], w_out[...], preferred_element_type=F32).astype(BF16)
    half[...] = packed[pl.ds(mine, 128), :]
    images = lax.broadcasted_iota(I32, (n, 128), 1).astype(F32)
    packed[:, :128] = jnp.where(seg_rows == images, 1.0, 0.0).astype(BF16)
    member[...] = packed[pl.ds(mine, 128), :128]


def keep_kernel(kept, w_out, keep):
    keep[...] = jnp.dot(kept[...], w_out[...], preferred_element_type=F32).astype(BF16)


def add_kernel(own, far, out):
    out[...] = (own[...].astype(F32) + far[...].astype(F32)).astype(BF16)


def mlp_share(normed, w1, w2):
    hidden = lax.dot_general(normed, w1, CONTRACT_LAST, preferred_element_type=F32)
    hidden = jax.nn.gelu(hidden, approximate=True).astype(BF16)
    return jnp.dot(hidden, w2, preferred_element_type=F32)


def near_kernel(half, own_sum, far_sum, w1, w2, resid, normed, part):
    base = half[...].astype(F32) + own_sum[...].astype(F32) + far_sum[...].astype(F32)
    resid[...] = base.astype(BF16)
    normed[...] = layer_norm(resid[...].astype(F32)).astype(BF16)
    part[...] = mlp_share(normed[...], w1[...], w2[...])


def far_kernel(resid, normed, part, text, w1, w2, first_out, second_out, share_out, total):
    total[...] = part[...] + mlp_share(normed[...], w1[...], w2[...])
    share_out[...] = total[...].astype(BF16)
    yl = lax.axis_index("yl")
    mine, other = pl.multiple_of(yl * 64, 64), pl.multiple_of(64 - yl * 64, 64)
    width = resid.shape[1]
    first_out[:64, :] = (total[pl.ds(mine, 64), :] + resid[pl.ds(mine, 64), :].astype(F32)).astype(BF16)
    first_out[64:, :] = jnp.concatenate([text[...].astype(F32), jnp.zeros((14, width), F32)], axis=0).astype(BF16)
    second_out[...] = total[pl.ds(other, 64), :].astype(BF16)


def pool_kernel(resid, own_share, far_share, member, pooled):
    layer = resid[...].astype(F32) + own_share[...].astype(F32) + far_share[...].astype(F32)
    normed = layer_norm(layer.astype(BF16).astype(F32))
    high = normed.astype(BF16)
    low = (normed - high.astype(F32)).astype(BF16)
    full = lax.dot_general(member[...], high, CONTRACT_FIRST, preferred_element_type=F32)
    full += lax.dot_general(member[...], low, CONTRACT_FIRST, preferred_element_type=F32)
    pooled[...] = full[:8]


def two_parts(values):
    high = values.astype(BF16).astype(F32)
    return jnp.concatenate([high, values - high], axis=0).astype(BF16)


def loss_kernel(where, counts, multiplier, shift, pooled_own, pooled_far, texts, grad_out):
    row8 = lax.broadcasted_iota(I32, (8, 1), 0)
    count = jnp.where(row8 == 0, counts[0, 0], counts[0, 1]).astype(F32)
    pooled = (pooled_own[...] + pooled_far[...]) / count
    norm_img = jnp.sqrt(jnp.sum(pooled * pooled, axis=1, keepdims=True) + 1e-06)
    unit = pooled / norm_img
    text = texts[...]
    square = text.astype(F32) * text.astype(F32)
    high = square.astype(BF16)
    low = (square - high.astype(F32)).astype(BF16)
    ones = jnp.ones((16, text.shape[1]), BF16)
    total = lax.dot_general(ones, high, CONTRACT_LAST, preferred_element_type=F32)
    total += lax.dot_general(ones, low, CONTRACT_LAST, preferred_element_type=F32)
    per_norm = lax.rsqrt(total[:8] + 1e-06)
    cosine = lax.dot_general(two_parts(unit), text, CONTRACT_LAST, preferred_element_type=F32)
    logits = multiplier[0] * (cosine[:8] + cosine[8:]) * per_norm + shift[0]
    column = lax.broadcasted_iota(I32, logits.shape, 1)
    text_index = (column >> 2) * (4 * N_XH) + (column & 3) + where[1]
    image_index = lax.broadcasted_iota(I32, logits.shape, 0) + where[0]
    slope = 1.0 / (1.0 + jnp.exp(-logits)) - jnp.where(text_index == image_index, 1.0, 0.0)
    grad = jnp.dot(two_parts(slope * per_norm), text, preferred_element_type=F32)
    grad = multiplier[0] * (grad[:8] + grad[8:])
    grad_out[...] = ((grad - unit * jnp.sum(unit * grad, axis=1, keepdims=True)) / norm_img)[:2].astype(BF16)


def place_kernel(gathered, rows_out, grad_out):
    planes, count, width = gathered.shape
    per_half, ring = planes // N_YH, count - 1
    row = lax.broadcasted_iota(I32, (128, 128), 0)
    column = lax.broadcasted_iota(I32, (128, 128), 1)
    plane, member = column // ring, column % ring
    target = (member >> 1) * 8 + (plane >> 1) * 4 + (member & 1) * 2 + (plane & 1)
    pick = jnp.where(row == target, 1.0, 0.0).astype(BF16)
    is_share = lax.broadcasted_iota(I32, (count, width), 0) == ring
    shares = [jnp.zeros((count, width), F32) for _ in range(2)]
    for half in range(N_YH):
        mine = [gathered[half * per_half + k] for k in range(per_half)]
        ordered = jnp.dot(pick, jnp.concatenate([p[:ring] for p in mine], axis=0), preferred_element_type=F32)
        rows_out[half * 128 : (half + 1) * 128, :] = ordered.astype(BF16)
        for k in range(per_half):
            shares[k % 2] += mine[k].astype(F32)
    grads = [jnp.sum(jnp.where(is_share, share, 0.0), axis=0, keepdims=True) for share in shares]
    grad_out[...] = jnp.concatenate(grads, axis=0)


def call(kernel, specs, outs, scratch=(), limit=None, flops=10**7, nbytes=10**6):
    many = isinstance(outs, list)
    return pl.pallas_call(
        kernel,
        in_specs=specs,
        out_specs=[VMEM] * len(outs) if many else VMEM,
        out_shape=outs,
        scratch_shapes=list(scratch),
        compiler_params=pltpu.CompilerParams(vmem_limit_bytes=limit),
        cost_estimate=pl.CostEstimate(flops=flops, bytes_accessed=nbytes, transcendentals=0),
    )


def per_device(rows_in, patch_counts, row_slots, w_qkv, w_out, w_fc1, w_fc2, text_embeds, multiplier, shift):
    row_count, width = rows_in.shape
    half_rows, quarter, ring = row_count // 2, row_count // 4, N_Z * N_XL
    shape = jax.ShapeDtypeStruct
    pair = [(0, 1), (1, 0)]

    send, kept, half, member = call(
        attend_kernel,
        [VMEM, VMEM, HBM, HBM, HBM],
        [
            pltpu.VMEM((half_rows, width), BF16),
            pltpu.VMEM((half_rows, w_out.shape[0]), BF16),
            pltpu.VMEM((half_rows, width), BF16),
            pltpu.VMEM((half_rows, 128), BF16),
        ],
        [
            pltpu.VMEM((row_count, width), BF16),
            pltpu.VMEM((row_count, w_out.shape[0]), BF16),
            pltpu.VMEM((row_count, width), BF16),
            pltpu.VMEM((w_qkv.shape[1], width), BF16),
            pltpu.VMEM(w_out.shape, BF16),
            pltpu.SemaphoreType.DMA((5,)),
        ],
        ATTEND_LIMIT,
        2 * 10**9,
        8 * 10**6,
    )(*(pltpu.with_memory_space_constraint(x, pltpu.HBM) for x in (patch_counts, row_slots, rows_in, w_qkv.T, w_out)))

    got = lax.ppermute(send, "core", pair)
    keep = call(keep_kernel, [VMEM] * 2, pltpu.VMEM((half_rows, width), BF16), limit=SMALL, flops=10**9)(
        kept, pltpu.with_memory_space_constraint(w_out, pltpu.HBM)
    )
    own_sum = call(add_kernel, [VMEM] * 2, shape((half_rows, width), BF16), limit=SMALL, flops=ADD_FLOPS)(keep, got)
    own_sum, far_w1, far_w2 = lax.optimization_barrier((own_sum, w_fc1.T, w_fc2))
    far_sum = lax.ppermute(own_sum, "yl", pair)
    far_w1 = lax.ppermute(far_w1, "core", pair)
    far_w2 = lax.ppermute(far_w2, "core", pair)

    resid, normed, part = call(
        near_kernel,
        [VMEM] * 5,
        [shape((half_rows, width), BF16), shape((half_rows, width), BF16), shape((half_rows, width), F32)],
        (),
        NEAR_LIMIT,
        NEAR_FLOPS,
        16 * 10**6,
    )(half, own_sum, far_sum, w_fc1.T, w_fc2)
    first, second, share = call(
        far_kernel,
        [VMEM] * 6,
        [shape((quarter + 16, width), BF16), shape((quarter, width), BF16), shape((half_rows, width), BF16)],
        [pltpu.VMEM((half_rows, width), F32)],
        BIG,
        4 * 10**9,
        16 * 10**6,
    )(resid, normed, part, text_embeds, far_w1, far_w2)

    first = swap_quarters(first)
    second = swap_quarters(second, 2)
    far_share = lax.ppermute(share, "yl", pair)
    layer = (first[:quarter].astype(F32) + second.astype(F32)).astype(BF16).reshape(ring, 2, width)
    text = jnp.broadcast_to(first[quarter : quarter + 2][None], layer.shape)
    arrived = lax.all_to_all(jnp.concatenate([layer, text], axis=1), RING, 0, 0, tiled=True)

    pooled = call(pool_kernel, [VMEM] * 4, shape((8, width), F32), limit=SMALL, flops=POOL_FLOPS)(resid, share, far_share, member)
    pooled_far = lax.ppermute(pooled, "core", pair)
    where = jnp.stack([lax.axis_index(DP) * 2, lax.axis_index("yl") * 128 + lax.axis_index("core") * 4]).astype(I32)
    grad = call(loss_kernel, [SMEM] * 4 + [VMEM] * 3, shape((2, width), BF16), limit=SMALL)(
        where, patch_counts, multiplier, shift, pooled, pooled_far, arrived[:, 2:].reshape(quarter, width)
    )

    bundle = jnp.concatenate([arrived[:, :2], grad[None]], axis=0)
    bundle = lax.all_gather(bundle, TP, axis=1, tiled=False)
    gathered = bundle.reshape(ring + 1, 8, width).transpose(1, 0, 2)
    return call(place_kernel, [VMEM], [shape((row_count, width), BF16), shape((2, width), F32)], limit=SMALL)(gathered)


def solution(mesh):
    fine = Mesh(mesh.devices.reshape(N_YH, N_Z, N_XH, N_XL, N_YL, N_CORE), DP + TP)
    placed = (
        P(DP, None),
        P(DP, None),
        P(DP, None),
        P(None, TP),
        P(TP, None),
        P(None, TP),
        P(TP, None),
        P(DP, None),
        P(),
        P(),
    )
    return jax.shard_map(per_device, mesh=fine, in_specs=placed, out_specs=(P(DP, None), P(DP, None)), check_vma=False)
```
